512 devices in a mesh: dp: 64 (over y, z), mp: 8 (over x, core).
Axes of the slice: x: 4, y: 8, z: 8, core: 2. Of those that a mesh axis runs over, the one named last changes fastest.
Arguments:
- activations: bfloat16 [16384, 4096], P('dp', 'mp'), may hold values from -6 to 6
- out_grad: bfloat16 [16384, 14336], P('dp', 'mp'), may hold values from -6 to 6
- row_blocks: int32 [112, 8], P('mp'), may hold values from 0 to 31, as said below
- doc_lengths: int32 [64, 4], P('dp'), may hold values from 0 to 256, as said below
Outputs:
- weight_grad: float32 [112, 1024, 128], P('mp', 'dp')
The draws below stay inside these ranges and needn't reach their ends.
Inputs may be any that keep to these rules, and one draw needn't show every extreme that they name: `row_blocks`: each row holds 8 distinct row-block indices. `doc_lengths`: the lengths of one index of dp sum to at most 256; at some index one document fills all 256 slots.
All inputs are finite; a program needn't handle non-finite values.
Results may differ from the reference program's by a relative error of at most 0.0003.
Values may be sent and summed in bfloat16 or wider, within the bound.
A program may use at most 64 MiB of HBM per device.

```python
import jax
import jax.numpy as jnp
from jax import lax

D = 4096
FF = 14336
BLOCK = 128
TOK_DEV = 256
DOCS = 4
RB = 32
NCB = 112
KNZ = 8
TOKENS = 16384
N_DP = 64


def draw_row_blocks(key, part):
    key = jax.random.fold_in(key, 11)
    keys = jax.random.split(key, NCB)
    picks = jax.vmap(lambda one: jax.random.permutation(one, RB)[:KNZ])(keys)
    return picks.astype(jnp.int32)


def draw_doc_lengths(key, part):
    key = jax.random.fold_in(key, 23)
    key_shift, key_cut, key_full, key_split = jax.random.split(key, 4)
    shift = jax.random.randint(key_shift, (N_DP,), 0, 3)
    base = jnp.int32(TOK_DEV) // jnp.left_shift(jnp.int32(1), shift.astype(jnp.int32))
    cut = jax.random.randint(key_cut, (N_DP,), 0, base // 4 + 1)
    totals = base - cut
    full = jax.random.randint(key_full, (), 0, N_DP)
    is_full = jnp.arange(N_DP) == full
    totals = jnp.where(is_full, jnp.int32(TOK_DEV), totals).astype(jnp.int32)
    cuts = jax.random.randint(key_split, (N_DP, DOCS - 1), 0, totals[:, None] + 1)
    cuts = jnp.where(is_full[:, None], jnp.int32(0), cuts).astype(jnp.int32)
    cuts = jnp.sort(cuts, axis=1)
    edges = jnp.concatenate([jnp.zeros((N_DP, 1), jnp.int32), cuts.astype(jnp.int32), totals[:, None]], axis=1)
    return (edges[:, 1:] - edges[:, :-1]).astype(jnp.int32)


def steps_of(own_key, shape, cuts, smallest, largest):
    factor_of, own = 1.0, jax.random.fold_in(own_key, 6)
    for axis_at, parts in cuts:
        draws = jnp.exp(jax.random.uniform(jax.random.fold_in(own, axis_at), (parts,), jnp.float32, smallest / len(cuts), largest / len(cuts)))
        factor_of = factor_of * jnp.repeat(draws, shape[axis_at] // parts).reshape([-1 if axis == axis_at else 1 for axis in range(len(shape))])
    return factor_of


def normal_values(own_key, shape, scale, bound, cuts=(), held_as=jnp.bfloat16):
    entries = jax.random.normal(own_key, shape, jnp.float32) * scale
    if len(cuts) > 0:
        entries = steps_of(own_key, shape, cuts, -0.22, 0.18) * entries
    return jnp.clip(entries, min=-bound, max=bound).astype(held_as)


def setup_inputs(seed: int = 0) -> dict:
    seeds = jax.random.split(jax.random.key(seed), 5)
    activations = normal_values(seeds[0], (TOKENS, D), 1.0, 6.0, ((0, 64), (1, 8)))
    out_grad = normal_values(seeds[1], (TOKENS, FF), 1.0, 6.0, ((0, 64), (1, 8)))
    row_blocks = draw_row_blocks(jax.random.fold_in(seeds[4], 71), 0)
    doc_lengths = draw_doc_lengths(jax.random.fold_in(seeds[4], 71), 0)
    return {"activations": activations, "out_grad": out_grad, "row_blocks": row_blocks, "doc_lengths": doc_lengths}


def reference(activations, out_grad, row_blocks, doc_lengths):
    live = lax.optimization_barrier(jnp.sum(doc_lengths, axis=1))
    slots = jnp.arange(TOK_DEV, dtype=jnp.int32)
    keep = (slots[None, :] < live[:, None]).reshape(-1)
    masked = jnp.where(keep[:, None], out_grad, jnp.zeros_like(out_grad))
    blocked = activations.reshape(activations.shape[0], RB, BLOCK)
    factor = jnp.float32(1.0) / jnp.sqrt(jnp.float32(TOKENS))

    def one_column(column):
        chosen = jnp.take(blocked, row_blocks[column], axis=1).reshape(activations.shape[0], KNZ * BLOCK)
        grads = lax.dynamic_slice_in_dim(masked, column * BLOCK, BLOCK, 1)
        total = lax.dot_general(chosen, grads, (((0,), (0,)), ((), ())), preferred_element_type=jnp.float32)
        return total * factor
    return lax.map(one_column, jnp.arange(NCB, dtype=jnp.int32))
```

```python
import functools
import math

import jax
import jax.numpy as jnp
from jax import lax
from jax.experimental import pallas as pl
from jax.experimental.pallas import tpu as pltpu
from jax.sharding import PartitionSpec as P

BLOCK = 128
CORES = 2
TOP = 32700.0
TINY = 1e-33


def quantize(x):
    peak = jnp.maximum(jnp.max(jnp.abs(x), axis=0, keepdims=True), TINY)
    return jnp.round(x * (TOP / peak)).astype(jnp.int32).astype(jnp.int16), peak * (1.0 / TOP)


def widen(q, scale):
    return q.astype(jnp.int32).astype(jnp.float32) * scale


def kernel(cfg, act, grad, rb, docs, out, feat, gm, sbuf, rbuf, ssc, rsc, s2buf, r2buf, s2sc, r2sc, fin,
           sib_s, sib_r, x_s, x_r, d_s, d_r, c_s, c_r, d2_s, d2_r, c2_s, c2_r):
    (ny, nz, nx, nb, knz, per_half, groups, factor) = cfg
    slots = act.shape[0]
    dp = lax.axis_index("dp")
    mp = lax.axis_index("mp")
    at = (dp // nz, lax.rem(dp, nz))
    sizes = (ny, nz)
    x, core = mp // CORES, lax.rem(mp, CORES)
    sibling = x * CORES + (1 - core)

    def along(axis, step):
        there = lax.rem(at[axis] + step + sizes[axis], sizes[axis])
        if axis == 0:
            return {"dp": there * nz + at[1], "mp": mp}
        return {"dp": at[0] * nz + there, "mp": mp}

    def x_device(step):
        return lax.rem(x + step + nx, nx) * CORES + core

    peers = [{"dp": dp, "mp": sibling}]
    if nx > 1:
        peers += [{"dp": dp, "mp": x_device(1)}, {"dp": dp, "mp": x_device(-1)}]
    for axis in (0, 1):
        peers += [along(axis, t) for t in range(1, sizes[axis])]
    barrier = pltpu.get_barrier_semaphore()
    for peer in peers:
        pl.semaphore_signal(barrier, inc=1, device_id=peer, device_id_type=pl.DeviceIdType.MESH)

    for b in range(nb):
        feat[mp * nb + b] = act[:, b * BLOCK:(b + 1) * BLOCK].T
    pl.semaphore_wait(barrier, len(peers))

    half = nb // 2

    def piece(device, part):
        return feat.at[pl.ds(device * nb + part * half, half)]

    def push(device, part, to, send, recv):
        return pltpu.make_async_remote_copy(
            src_ref=piece(device, part), dst_ref=piece(device, part), send_sem=send, recv_sem=recv,
            device_id={"dp": dp, "mp": to}, device_id_type=pl.DeviceIdType.MESH)

    def share(hop, device, part):
        return push(device, part, sibling, sib_s.at[hop, part], sib_r.at[hop, part])

    started = []

    def go(copy):
        copy.start()
        started.append(copy)

    if nx > 1:
        right, left, far = x_device(1), x_device(-1), x_device(2)
        go(push(mp, 0, right, x_s.at[0, 0], x_r.at[0, 0]))
        go(push(mp, 1, left, x_s.at[1, 0], x_r.at[1, 0]))
        go(push(mp, 1, right, x_s.at[0, 1], x_r.at[0, 1]))
        go(push(mp, 0, left, x_s.at[1, 1], x_r.at[1, 1]))
    go(share(0, mp, 0))
    go(share(0, mp, 1))

    live = docs[0, 0]
    for d in range(1, docs.shape[1]):
        live = live + docs[0, d]
    keep = lax.broadcasted_iota(jnp.int32, (slots, BLOCK), 0) < live
    for c in range(2 * per_half):
        part = grad[:, c * BLOCK:(c + 1) * BLOCK]
        gm[c] = jnp.where(keep, part, jnp.zeros_like(part))

    if nx > 1:
        push(left, 0, right, x_s.at[0, 0], x_r.at[0, 0]).wait_recv()
        go(push(left, 0, right, x_s.at[0, 2], x_r.at[0, 2]))
        go(share(1, left, 0))
        push(right, 1, left, x_s.at[1, 0], x_r.at[1, 0]).wait_recv()
        go(push(right, 1, left, x_s.at[1, 2], x_r.at[1, 2]))
        go(share(2, right, 1))
        push(left, 1, right, x_s.at[0, 1], x_r.at[0, 1]).wait_recv()
        go(share(1, left, 1))
        push(right, 0, left, x_s.at[1, 1], x_r.at[1, 1]).wait_recv()
        go(share(2, right, 0))
        push(far, 0, right, x_s.at[0, 2], x_r.at[0, 2]).wait_recv()
        go(share(3, far, 0))
        push(far, 1, left, x_s.at[1, 2], x_r.at[1, 2]).wait_recv()
        go(share(3, far, 1))
    for hop in range(4 if nx > 1 else 1):
        for part in (0, 1):
            share(hop, mp, part).wait_recv()

    rows = BLOCK // nz if nz > 1 else BLOCK // 1
    sub = (BLOCK // nz, BLOCK // ny)

    def local(h, c, owner):
        if h == 0:
            lhs = feat[rb[c, owner]]
        else:
            span = BLOCK // nz
            lhs = jnp.concatenate(
                [feat[rb[per_half + c, k], pl.ds(pl.multiple_of(owner * span, span), span), :] for k in range(knz)], axis=0)
        return jnp.dot(lhs, gm[h * per_half + c], preferred_element_type=jnp.float32)

    def message(h, way, s, g):
        lo, hi = groups[g]
        n = sizes[h]
        where = pl.ds(0, BLOCK)
        if s == 0:
            where = pl.ds(way * (BLOCK // 2), BLOCK // 2)
        to = along(h, 1 - 2 * way)
        data = pltpu.make_async_remote_copy(
            src_ref=sbuf.at[h, way, s, pl.ds(lo, hi - lo), where], dst_ref=rbuf.at[h, way, s, pl.ds(lo, hi - lo), where],
            send_sem=d_s.at[h, way, s, g], recv_sem=d_r.at[h, way, s, g],
            device_id=to, device_id_type=pl.DeviceIdType.MESH)
        scale = pltpu.make_async_remote_copy(
            src_ref=ssc.at[h, way, s, g], dst_ref=rsc.at[h, way, s, g],
            send_sem=c_s.at[h, way, s, g], recv_sem=c_r.at[h, way, s, g],
            device_id=to, device_id_type=pl.DeviceIdType.MESH)
        return data, scale

    def arrived(h, way, s, g):
        for copy in message(h, way, s, g):
            copy.wait_recv()

    def add_arrived(x, h, way, s, g, c):
        lo = groups[g][0]
        scale = rsc[h, way, s, g, pl.ds(c - lo, 1), :]
        if s > 0:
            return x + widen(rbuf[h, way, s, c], scale)
        mid = BLOCK // 2
        here = widen(rbuf[h, way, s, c, pl.ds(way * mid, mid), :], scale)
        if way == 0:
            return jnp.concatenate([x[:mid] + here, x[mid:]], axis=0)
        return jnp.concatenate([x[:mid], x[mid:] + here], axis=0)

    def first_step(h, g):
        lo, hi = groups[g]
        n = sizes[h]
        owner = lax.rem(at[h] + n // 2, n)

        def column(c, _):
            x = local(h, c, owner)
            mid = BLOCK // 2
            for way in (0, 1):
                q, scale = quantize(x[way * mid:(way + 1) * mid])
                sbuf[h, way, 0, c, pl.ds(way * mid, mid), :] = q
                ssc[h, way, 0, g, pl.ds(c - lo, 1), :] = scale
            return 0
        lax.fori_loop(lo, hi, column, 0)
        for way in (0, 1):
            for copy in message(h, way, 0, g):
                go(copy)

    def later_step(h, way, s, g):
        lo, hi = groups[g]
        n = sizes[h]
        distance = n // 2 - s
        owner = lax.rem(at[h] + (1 - 2 * way) * distance + n, n)
        arrived(h, way, s - 1, g)

        def column(c, _):
            x = add_arrived(local(h, c, owner), h, way, s - 1, g, c)
            q, scale = quantize(x)
            sbuf[h, way, s, c] = q
            ssc[h, way, s, g, pl.ds(c - lo, 1), :] = scale
            return 0
        lax.fori_loop(lo, hi, column, 0)
        for copy in message(h, way, s, g):
            go(copy)

    def second(h, t, g):
        lo, hi = groups[g]
        axis = 1 - h
        to = along(axis, t)
        there = lax.rem(at[axis] + t, sizes[axis])
        data = pltpu.make_async_remote_copy(
            src_ref=s2buf.at[h, there, pl.ds(lo, hi - lo)], dst_ref=r2buf.at[h, t, pl.ds(lo, hi - lo)],
            send_sem=d2_s.at[h, t, g], recv_sem=d2_r.at[h, t, g],
            device_id=to, device_id_type=pl.DeviceIdType.MESH)
        scale = pltpu.make_async_remote_copy(
            src_ref=s2sc.at[h, g], dst_ref=r2sc.at[h, t, g],
            send_sem=c2_s.at[h, t, g], recv_sem=c2_r.at[h, t, g],
            device_id=to, device_id_type=pl.DeviceIdType.MESH)
        return data, scale

    def own_step(h, g):
        lo, hi = groups[g]
        n = sizes[h]
        last = n // 2 - 1
        if n > 1:
            for way in (0, 1):
                arrived(h, way, last, g)

        def column(c, _):
            x = local(h, c, at[h])
            if n > 1:
                for way in (0, 1):
                    x = add_arrived(x, h, way, last, g, c)
            fin[h, c] = x
            q, scale = quantize(x)
            span = BLOCK // sizes[1 - h]
            for o in range(sizes[1 - h]):
                s2buf[h, o, c] = q[o * span:(o + 1) * span]
            s2sc[h, g, pl.ds(c - lo, 1), :] = scale
            return 0
        lax.fori_loop(lo, hi, column, 0)
        for t in range(1, sizes[1 - h]):
            for copy in second(h, t, g):
                go(copy)

    def finish(h, g):
        lo, hi = groups[g]
        n = sizes[1 - h]
        span = BLOCK // n
        for t in range(1, n):
            for copy in second(h, t, g):
                copy.wait_recv()

        def column(c, _):
            x = fin[h, c, pl.ds(pl.multiple_of(at[1 - h] * span, span), span), :]
            for t in range(1, n):
                x = x + widen(r2buf[h, t, c], r2sc[h, t, g, pl.ds(c - lo, 1), :])
            out[h * per_half + c] = x * factor
            return 0
        lax.fori_loop(lo, hi, column, 0)

    for s in range(max(sizes) // 2):
        for g in range(len(groups)):
            for h in (0, 1):
                if s >= sizes[h] // 2:
                    continue
                if s == 0:
                    first_step(h, g)
                else:
                    for way in (0, 1):
                        later_step(h, way, s, g)
    for g in range(len(groups)):
        for h in (0, 1):
            own_step(h, g)
    for g in range(len(groups)):
        for h in (0, 1):
            finish(h, g)
    for copy in started:
        copy.wait_send()


def shards(ny, nz, nx, groups, activations, out_grad, row_blocks, doc_lengths):
    slots = activations.shape[0]
    nb = activations.shape[1] // BLOCK
    columns, knz = row_blocks.shape
    per_half = columns // 2
    dp = ny * nz
    factor = 1.0 / math.sqrt(slots * dp)
    cfg = (ny, nz, nx, nb, knz, per_half, groups, factor)
    blocks = nb * nx * CORES
    steps = max(1, max(ny, nz) // 2)
    ng = len(groups)
    span = BLOCK // min(ny, nz)
    most = max(ny, nz)
    vmem = pl.BlockSpec(memory_space=pltpu.VMEM)
    smem = pl.BlockSpec(memory_space=pltpu.SMEM)
    dma = pltpu.SemaphoreType.DMA
    return pl.pallas_call(
        functools.partial(kernel, cfg),
        out_shape=jax.ShapeDtypeStruct((columns, knz * BLOCK // dp, BLOCK), jnp.float32),
        in_specs=[vmem, vmem, smem, smem],
        out_specs=vmem,
        scratch_shapes=[
            pltpu.VMEM((blocks, BLOCK, slots), jnp.bfloat16),
            pltpu.VMEM((columns, slots, BLOCK), jnp.bfloat16),
            pltpu.VMEM((2, 2, steps, per_half, BLOCK, BLOCK), jnp.int16),
            pltpu.VMEM((2, 2, steps, per_half, BLOCK, BLOCK), jnp.int16),
            pltpu.VMEM((2, 2, steps, ng, 8, BLOCK), jnp.float32),
            pltpu.VMEM((2, 2, steps, ng, 8, BLOCK), jnp.float32),
            pltpu.VMEM((2, most, per_half, span, BLOCK), jnp.int16),
            pltpu.VMEM((2, most, per_half, span, BLOCK), jnp.int16),
            pltpu.VMEM((2, ng, 8, BLOCK), jnp.float32),
            pltpu.VMEM((2, most, ng, 8, BLOCK), jnp.float32),
            pltpu.VMEM((2, per_half, BLOCK, BLOCK), jnp.float32),
            dma((4, 2)), dma((4, 2)),
            dma((2, 3)), dma((2, 3)),
            dma((2, 2, steps, ng)), dma((2, 2, steps, ng)),
            dma((2, 2, steps, ng)), dma((2, 2, steps, ng)),
            dma((2, most, ng)), dma((2, most, ng)),
            dma((2, most, ng)), dma((2, most, ng)),
        ],
        compiler_params=pltpu.CompilerParams(
            collective_id=0, has_side_effects=True, vmem_limit_bytes=40 * 2**20),
    )(activations, out_grad, row_blocks, doc_lengths)


def solution(mesh):
    dp, mp = mesh.shape["dp"], mesh.shape["mp"]
    nz = math.isqrt(dp)
    ny = dp // nz
    body = functools.partial(shards, ny, nz, mp // CORES, ((0, 2), (2, 4), (4, 7)))
    in_specs = (P("dp", "mp"), P("dp", "mp"), P("mp", None), P("dp", None))
    return jax.shard_map(body, mesh=mesh, in_specs=in_specs, out_specs=P("mp", "dp", None), check_vma=False)
```

```python
import functools
import math

import jax
import jax.numpy as jnp
from jax import lax
from jax.experimental import pallas as pl
from jax.experimental.pallas import tpu as pltpu
from jax.sharding import PartitionSpec as P

BLOCK = 128
CORES = 2
CODES = 16
FINE = 64.0
TOP = 32700.0
TINY = 1e-33
GROUPS = ((0, 2), (2, 4), (4, 7))
MESH = pl.DeviceIdType.MESH


def quantize(x):
    peak = jnp.maximum(jnp.max(jnp.abs(x), axis=0, keepdims=True), TINY)
    code = jnp.ceil(jnp.log2(peak * (1.0 / TOP)) * FINE)
    q = jnp.round(x * jnp.exp2(code * (-1.0 / FINE)))
    return q.astype(jnp.int32).astype(jnp.int16), code


def code_rows(codes):
    rows = jnp.concatenate(codes + [jnp.zeros((CODES - len(codes), BLOCK), jnp.float32)], axis=0)
    return rows.astype(jnp.int32).astype(jnp.int16)


def scales_of(tile):
    return jnp.exp2(tile.astype(jnp.int32).astype(jnp.float32) * (1.0 / FINE))


def widen(q, scale):
    return q.astype(jnp.int32).astype(jnp.float32) * scale


def first_way(g):
    return 1 if g == len(GROUPS) - 1 else 0


def kernel(cfg, act_hbm, grad_hbm, rb_hbm, docs_hbm, out, act, grad, rb, docs, feat, gm, part, sn, rn, s2, r2, c2, rc2, fin,
           in_sem, x_r, sib_r, m_r, m2_r, send_sem):
    n, nx, nb, knz, per_half, groups, factor = cfg
    slots = act.shape[0]
    span = BLOCK // n
    steps = n // 2
    dp = lax.axis_index("dp")
    mp = lax.axis_index("mp")
    at = (dp // n, lax.rem(dp, n))
    x, core = mp // CORES, lax.rem(mp, CORES)
    sibling = x * CORES + (1 - core)

    def along(axis, step):
        there = lax.rem(at[axis] + step + n, n)
        if axis == 0:
            return {"dp": there * n + at[1], "mp": mp}
        return {"dp": at[0] * n + there, "mp": mp}

    def x_device(step):
        return lax.rem(x + step + nx, nx) * CORES + core

    peers = [{"dp": dp, "mp": sibling}]
    if nx > 1:
        peers += [{"dp": dp, "mp": x_device(1)}, {"dp": dp, "mp": x_device(-1)}]
    for axis in (0, 1):
        peers += [along(axis, t) for t in range(1, n)]
    barrier = pltpu.get_barrier_semaphore()
    for peer in peers:
        pl.semaphore_signal(barrier, inc=1, device_id=peer, device_id_type=MESH)

    loads = [pltpu.make_async_copy(a, b, in_sem.at[i])
             for i, (a, b) in enumerate(((act_hbm, act), (docs_hbm, docs), (rb_hbm, rb), (grad_hbm, grad)))]
    for load in loads:
        load.start()
    loads[0].wait()
    for b in range(nb):
        feat[mp * nb + b] = act[:, b * BLOCK:(b + 1) * BLOCK].T
    pl.semaphore_wait(barrier, len(peers))

    def push(block, to, recv, send):
        return pltpu.make_async_remote_copy(
            src_ref=feat.at[block], dst_ref=feat.at[block], send_sem=send, recv_sem=recv,
            device_id={"dp": dp, "mp": to}, device_id_type=MESH)

    def share(block):
        push(block, sibling, sib_r.at[0], send_sem.at[1]).start()

    half = nb // 2
    if nx > 1:
        right, left, far = x_device(1), x_device(-1), x_device(2)

    def to_right(block, i):
        return push(block, right, x_r.at[0, i], send_sem.at[0])

    def to_left(block, i):
        return push(block, left, x_r.at[1, i], send_sem.at[0])

    turned = [*range(half, nb), *range(half)]
    if nx > 1:
        for b, e in zip(range(nb), turned):
            to_right(mp * nb + b, b).start()
            to_left(mp * nb + e, e).start()
    for b in range(nb):
        share(mp * nb + b)

    for load in loads[1:]:
        load.wait()
    live = docs[0, 0]
    for d in range(1, docs.shape[1]):
        live = live + docs[0, d]
    keep = lax.broadcasted_iota(jnp.int32, (slots, BLOCK), 0) < live
    for c in range(2 * per_half):
        tile = grad[:, c * BLOCK:(c + 1) * BLOCK]
        gm[c] = jnp.where(keep, tile, jnp.zeros_like(tile))

    if nx > 1:
        for b, e in zip(range(nb), turned):
            to_right(left * nb + b, b).wait_recv()
            if b < half:
                to_right(left * nb + b, nb + b).start()
            share(left * nb + b)
            to_left(right * nb + e, e).wait_recv()
            if e >= half:
                to_left(right * nb + e, half + e).start()
            share(right * nb + e)
        for b in range(half):
            to_right(far * nb + b, nb + b).wait_recv()
            share(far * nb + b)
            to_left(far * nb + half + b, nb + b).wait_recv()
            share(far * nb + half + b)
    everything = feat.at[pl.ds(0, nb * nx)]
    pltpu.make_async_remote_copy(
        src_ref=everything, dst_ref=everything, send_sem=send_sem.at[1], recv_sem=sib_r.at[0],
        device_id={"dp": dp, "mp": sibling}, device_id_type=MESH).wait_recv()

    def chunk(h, c, owner):
        if h == 0:
            return part[c, owner]
        wide = part[per_half + c, :, pl.ds(pl.multiple_of(owner * span, span), span), :]
        return wide.reshape(BLOCK, BLOCK)

    def hops(way, g):
        return steps if way == first_way(g) else n - 1 - steps

    plan, total = {}, 0
    for way in (0, 1):
        for g, (lo, hi) in enumerate(groups):
            for d in range(1, hops(way, g) + 1):
                for h in (0, 1):
                    plan[h, way, d, g] = (len(plan), total)
                    total += (hi - lo) * BLOCK + CODES

    def message(h, way, d, g):
        lo, hi = groups[g]
        index, first = plan[h, way, d, g]
        there = pl.ds(first, (hi - lo) * BLOCK + CODES)
        return pltpu.make_async_remote_copy(
            src_ref=sn.at[there], dst_ref=rn.at[there], send_sem=send_sem.at[2], recv_sem=m_r.at[index],
            device_id=along(h, 1 - 2 * way), device_id_type=MESH)

    def add_arrived(values, h, way, d, g):
        message(h, way, d, g).wait_recv()
        first = plan[h, way, d, g][1]
        last = first + len(values) * BLOCK
        scales = scales_of(rn[last:last + CODES, :])
        return [v + widen(rn[first + j * BLOCK:first + (j + 1) * BLOCK, :], scales[j:j + 1]) for j, v in enumerate(values)]

    def put(h, way, d, g, values):
        first = plan[h, way, d, g][1]
        last = first + len(values) * BLOCK
        codes = []
        for j, value in enumerate(values):
            q, code = quantize(value)
            sn[first + j * BLOCK:first + (j + 1) * BLOCK, :] = q
            codes.append(code)
        sn[last:last + CODES, :] = code_rows(codes)
        message(h, way, d, g).start()

    def products(h, g):
        for c in range(*groups[g]):
            column = h * per_half + c
            lhs = jnp.concatenate([feat[rb[column, k]] for k in range(knz)], axis=0)
            sums = jnp.dot(lhs, gm[column], preferred_element_type=jnp.float32)
            part[column] = sums.reshape(knz, BLOCK, BLOCK)

    def step(h, way, r, g):
        d = hops(way, g) - r
        if d < 1:
            return
        owner = lax.rem(at[h] + (1 - 2 * way) * d + n, n)
        values = [chunk(h, c, owner) for c in range(*groups[g])]
        if r > 0:
            values = add_arrived(values, h, way, d + 1, g)
        put(h, way, d, g, values)

    def second(h, t, g):
        lo, hi = groups[g]
        there = lax.rem(at[1 - h] + t, n)
        rows, scale_rows = pl.ds(lo * span, (hi - lo) * span), pl.ds(0, hi - lo)
        to = along(1 - h, t)
        data = pltpu.make_async_remote_copy(
            src_ref=s2.at[h, there, rows], dst_ref=r2.at[h, t, rows],
            send_sem=send_sem.at[3], recv_sem=m2_r.at[0, h, g], device_id=to, device_id_type=MESH)
        scale = pltpu.make_async_remote_copy(
            src_ref=c2.at[h, g, scale_rows], dst_ref=rc2.at[h, t, g, scale_rows],
            send_sem=send_sem.at[4], recv_sem=m2_r.at[1, h, g], device_id=to, device_id_type=MESH)
        return scale, data

    def own_step(h, g):
        lo, hi = groups[g]
        values = [chunk(h, c, at[h]) for c in range(lo, hi)]
        for way in (0, 1):
            if hops(way, g) > 0:
                values = add_arrived(values, h, way, 1, g)
        for j, value in enumerate(values):
            fin[h, lo + j] = value
            peak = jnp.maximum(jnp.max(jnp.abs(value), axis=0, keepdims=True), TINY)
            q = jnp.round(value * (TOP / peak)).astype(jnp.int32).astype(jnp.int16)
            for o in range(n):
                s2[h, o, (lo + j) * span:(lo + j + 1) * span, :] = q[o * span:(o + 1) * span]
            c2[h, g, j:j + 1, :] = peak * (1.0 / TOP)
        for t in sorted(range(1, n), key=lambda t: -min(t, n - t)):
            for copy in second(h, t, g):
                copy.start()

    def finish(h, g):
        lo, hi = groups[g]
        mine = pl.ds(pl.multiple_of(at[1 - h] * span, span), span)
        values = [fin[h, c, mine, :] for c in range(lo, hi)]
        if n > 1:
            others = pl.ds(1, n - 1)
            arrivals = (rc2.at[h, others, g, pl.ds(0, hi - lo)], r2.at[h, others, pl.ds(lo * span, (hi - lo) * span)])
            for i, ref in ((1, arrivals[0]), (0, arrivals[1])):
                pltpu.make_async_remote_copy(
                    src_ref=ref, dst_ref=ref, send_sem=send_sem.at[3 + i], recv_sem=m2_r.at[i, h, g],
                    device_id=along(1 - h, 1), device_id_type=MESH).wait_recv()
        for t in range(1, n):
            for j in range(hi - lo):
                rows = slice((lo + j) * span, (lo + j + 1) * span)
                values[j] = values[j] + widen(r2[h, t, rows, :], rc2[h, t, g, j:j + 1, :])
        for j in range(hi - lo):
            out[h * per_half + lo + j] = values[j] * factor

    order = [(h, g) for g in range(len(groups)) for h in (0, 1)]
    for r in range(max(1, steps)):
        for h, g in order:
            if r == 0:
                products(h, g)
            for way in (first_way(g), 1 - first_way(g)):
                step(h, way, r, g)
    for h, g in order:
        own_step(h, g)
    for h, g in order:
        finish(h, g)

    def sent(ref, i):
        pltpu.make_async_remote_copy(
            src_ref=ref, dst_ref=ref, send_sem=send_sem.at[i], recv_sem=sib_r.at[0],
            device_id={"dp": dp, "mp": sibling}, device_id_type=MESH).wait_send()

    if nx > 1:
        sent(feat.at[pl.ds(0, 3 * nb)], 0)
    sent(everything, 1)
    if n > 1:
        sent(sn, 2)
        sent(s2.at[:, pl.ds(1, n - 1)], 3)
        for g, (lo, hi) in enumerate(groups):
            sent(rc2.at[:, pl.ds(1, n - 1), g, pl.ds(0, hi - lo)], 4)


def shards(n, nx, groups, activations, out_grad, row_blocks, doc_lengths):
    slots = activations.shape[0]
    nb = activations.shape[1] // BLOCK
    columns, knz = row_blocks.shape
    per_half = columns // 2
    factor = 1.0 / math.sqrt(slots * n * n)
    cfg = (n, nx, nb, knz, per_half, groups, factor)
    ng = len(groups)
    span = BLOCK // n
    dma = pltpu.SemaphoreType.DMA
    anywhere = pl.BlockSpec(memory_space=pl.ANY)
    chains = [(hi - lo, n // 2 if way == first_way(g) else n - 1 - n // 2)
              for g, (lo, hi) in enumerate(groups) for way in (0, 1) for h in (0, 1)]
    messages = max(1, sum(hops for _, hops in chains))
    rows = max(CODES, sum(hops * (wide * BLOCK + CODES) for wide, hops in chains))
    return pl.pallas_call(
        functools.partial(kernel, cfg),
        out_shape=jax.ShapeDtypeStruct((columns, span * knz // n, BLOCK), jnp.float32),
        in_specs=[anywhere] * 4,
        out_specs=pl.BlockSpec(memory_space=pltpu.VMEM),
        scratch_shapes=[
            pltpu.VMEM(activations.shape, jnp.bfloat16),
            pltpu.VMEM(out_grad.shape, jnp.bfloat16),
            pltpu.SMEM(row_blocks.shape, jnp.int32),
            pltpu.SMEM(doc_lengths.shape, jnp.int32),
            pltpu.VMEM((nb * nx * CORES, BLOCK, slots), jnp.bfloat16),
            pltpu.VMEM((columns, slots, BLOCK), jnp.bfloat16),
            pltpu.VMEM((columns, knz, BLOCK, BLOCK), jnp.float32),
            pltpu.VMEM((rows, BLOCK), jnp.int16),
            pltpu.VMEM((rows, BLOCK), jnp.int16),
            pltpu.VMEM((2, n, per_half * span, BLOCK), jnp.int16),
            pltpu.VMEM((2, n, per_half * span, BLOCK), jnp.int16),
            pltpu.VMEM((2, ng, 8, BLOCK), jnp.float32),
            pltpu.VMEM((2, n, ng, 8, BLOCK), jnp.float32),
            pltpu.VMEM((2, per_half, BLOCK, BLOCK), jnp.float32),
            dma((4,)),
            dma((2, nb + nb // 2)),
            dma((1,)),
            dma((messages,)),
            dma((2, 2, ng)),
            dma((5,)),
        ],
        compiler_params=pltpu.CompilerParams(
            collective_id=0, has_side_effects=True, vmem_limit_bytes=56 * 2**20),
    )(activations, out_grad, row_blocks, doc_lengths)


def solution(mesh):
    n = math.isqrt(mesh.shape["dp"])
    body = functools.partial(shards, n, mesh.shape["mp"] // CORES, GROUPS)
    in_specs = (P("dp", "mp"), P("dp", "mp"), P("mp", None), P("dp", None))
    return jax.shard_map(body, mesh=mesh, in_specs=in_specs, out_specs=P("mp", "dp", None), check_vma=False)
```

```python
import functools
import math

import jax
import jax.numpy as jnp
from jax import lax
from jax.experimental import pallas as pl
from jax.experimental.pallas import tpu as pltpu
from jax.sharding import PartitionSpec as P

BLOCK = 128
CORES = 2
TOP = 32700.0
TINY = 1e-33
GROUPS = ((0, 1), (1, 2), (2, 3), (3, 5), (5, 7))
ORDER = (
    (0,), (1, 0, 3), (0, 0, 4), (1,), (1, 1, 4), (0, 1, 3), (2,), (3,), (1, 3, 4), (0, 2, 4), (4,), (0, 4, 4),
    (1, 2, 3), (1, 0, 2), (0, 0, 3), (1, 1, 3), (0, 3, 3), (1, 4, 3), (0, 2, 3), (1, 3, 3), (0, 1, 2), (0, 4, 3),
    (1, 2, 2), (1, 1, 2), (0, 0, 2), (1, 0, 1), (0, 3, 2), (1, 4, 2), (0, 1, 1), (1, 3, 2), (0, 2, 2), (0, 4, 2),
    (1, 1, 1), (1, 2, 1), (0, 0, 1), (0, 3, 1), (1, 4, 1), (0, 2, 1), (1, 3, 1), (1, 0), (0, 4, 1), (0, 0), (2, 0),
    (3, 0), (4, 0),
)
MESH = pl.DeviceIdType.MESH


def quantize(x):
    peak = jnp.maximum(jnp.max(jnp.abs(x), axis=0, keepdims=True), TINY)
    return jnp.round(x * (TOP / peak)).astype(jnp.int32).astype(jnp.int16), peak * (1.0 / TOP)


def widen(q, scale):
    return q.astype(jnp.int32).astype(jnp.float32) * scale


def hops_of(n, way, g):
    return n // 2 if way == g % 2 else n - 1 - n // 2


def order_of(n, groups):
    if n == 8 and groups == GROUPS:
        return ORDER
    order = []
    for r in range(max(1, n // 2)):
        for g in range(len(groups)):
            order += [(g,)] if r == 0 else []
            order += [(way, g, hops_of(n, way, g) - r) for way in (g % 2, 1 - g % 2) if hops_of(n, way, g) > r]
    return order + [(g, 0) for g in range(len(groups))]


def kernel(cfg, act_hbm, grad_hbm, rb_hbm, docs_hbm, out, act, grad, rb, docs, feat, gm, part, sn, rn, cn, rcn, s2, r2, c2, rc2, fin,
           in_sem, x_r, sib_r, m_r, m2_r, send_sem):
    n, nx, nb, knz, per_half, groups, factor = cfg
    slots = act.shape[0]
    span = BLOCK // n
    mid = BLOCK // 2
    dp = lax.axis_index("dp")
    mp = lax.axis_index("mp")
    at = (dp // n, lax.rem(dp, n))
    x, core = mp // CORES, lax.rem(mp, CORES)
    sibling = x * CORES + (1 - core)

    def along(axis, step):
        there = lax.rem(at[axis] + step + n, n)
        if axis == 0:
            return {"dp": there * n + at[1], "mp": mp}
        return {"dp": at[0] * n + there, "mp": mp}

    def x_device(step):
        return lax.rem(x + step + nx, nx) * CORES + core

    peers = [{"dp": dp, "mp": sibling}]
    if nx > 1:
        peers += [{"dp": dp, "mp": x_device(1)}, {"dp": dp, "mp": x_device(-1)}]
    for axis in (0, 1):
        peers += [along(axis, t) for t in range(1, n)]
    barrier = pltpu.get_barrier_semaphore()
    for peer in peers:
        pl.semaphore_signal(barrier, inc=1, device_id=peer, device_id_type=MESH)

    loads = [pltpu.make_async_copy(a, b, in_sem.at[i])
             for i, (a, b) in enumerate(((act_hbm, act), (docs_hbm, docs), (rb_hbm, rb), (grad_hbm, grad)))]
    for load in loads:
        load.start()
    loads[0].wait()
    for b in range(nb):
        feat[mp * nb + b] = act[:, b * BLOCK:(b + 1) * BLOCK].T
    pl.semaphore_wait(barrier, len(peers))

    def push(block, to, recv, send):
        return pltpu.make_async_remote_copy(
            src_ref=feat.at[block], dst_ref=feat.at[block], send_sem=send, recv_sem=recv,
            device_id={"dp": dp, "mp": to}, device_id_type=MESH)

    def share(block):
        push(block, sibling, sib_r.at[0], send_sem.at[1]).start()

    half = nb // 2
    if nx > 1:
        right, left, far = x_device(1), x_device(-1), x_device(2)

    def to_right(block, i):
        return push(block, right, x_r.at[0, i], send_sem.at[0])

    def to_left(block, i):
        return push(block, left, x_r.at[1, i], send_sem.at[0])

    turned = [*range(half, nb), *range(half)]
    if nx > 1:
        for b, e in zip(range(nb), turned):
            to_right(mp * nb + b, b).start()
            to_left(mp * nb + e, e).start()
    for b in range(nb):
        share(mp * nb + b)

    for load in loads[1:]:
        load.wait()
    live = docs[0, 0]
    for d in range(1, docs.shape[1]):
        live = live + docs[0, d]
    keep = lax.broadcasted_iota(jnp.int32, (slots, BLOCK), 0) < live
    for c in range(2 * per_half):
        tile = grad[:, c * BLOCK:(c + 1) * BLOCK]
        gm[c] = jnp.where(keep, tile, jnp.zeros_like(tile))

    if nx > 1:
        for b, e in zip(range(nb), turned):
            to_right(left * nb + b, b).wait_recv()
            if b < half:
                to_right(left * nb + b, nb + b).start()
            share(left * nb + b)
            to_left(right * nb + e, e).wait_recv()
            if e >= half:
                to_left(right * nb + e, half + e).start()
            share(right * nb + e)
        for b in range(half):
            to_right(far * nb + b, nb + b).wait_recv()
            share(far * nb + b)
            to_left(far * nb + half + b, nb + b).wait_recv()
            share(far * nb + half + b)
    everything = feat.at[pl.ds(0, nb * nx)]
    pltpu.make_async_remote_copy(
        src_ref=everything, dst_ref=everything, send_sem=send_sem.at[1], recv_sem=sib_r.at[0],
        device_id={"dp": dp, "mp": sibling}, device_id_type=MESH).wait_recv()

    def chunk(h, c, owner):
        if h == 0:
            return part[c, owner]
        wide = part[per_half + c, :, pl.ds(pl.multiple_of(owner * span, span), span), :]
        return wide.reshape(BLOCK, BLOCK)

    plan, count = {}, 0
    for way in (0, 1):
        for g, (lo, hi) in enumerate(groups):
            for d in range(1, hops_of(n, way, g) + 1):
                for h in (0, 1):
                    plan[h, way, d, g] = (len(plan), count)
                    count += hi - lo

    def remote(src, dst, send, recv, to):
        return pltpu.make_async_remote_copy(
            src_ref=src, dst_ref=dst, send_sem=send_sem.at[send], recv_sem=recv, device_id=to, device_id_type=MESH)

    def message(h, way, d, g):
        lo, hi = groups[g]
        index, first = plan[h, way, d, g]
        to = along(h, 1 - 2 * way)
        rows, scales = pl.ds(first * BLOCK, (hi - lo) * BLOCK), pl.ds(first, hi - lo)
        return (remote(cn.at[scales], rcn.at[scales], 4, m_r.at[index], to),
                remote(sn.at[rows], rn.at[rows], 2, m_r.at[index], to))

    def add_arrived(values, h, way, d, g):
        index, first = plan[h, way, d, g]
        both = part.at[pl.ds(0, len(values)), 0, pl.ds(0, mid + 1)]
        remote(both, both, 2, m_r.at[index], along(h, 1 - 2 * way)).wait_recv()
        return [v + widen(rn[(first + j) * BLOCK:(first + j + 1) * BLOCK, :], rcn[first + j:first + j + 1, :])
                for j, v in enumerate(values)]

    def put(h, way, d, g, values):
        first = plan[h, way, d, g][1]
        for j, value in enumerate(values):
            q, scale = quantize(value)
            sn[(first + j) * BLOCK:(first + j + 1) * BLOCK, :] = q
            cn[first + j:first + j + 1, :] = scale
        for copy in message(h, way, d, g):
            copy.start()

    def products(h, g):
        for c in range(*groups[g]):
            column = h * per_half + c
            lhs = jnp.concatenate([feat[rb[k, column]] for k in range(knz)], axis=0)
            sums = jnp.dot(lhs, gm[column], preferred_element_type=jnp.float32)
            part[column] = sums.reshape(knz, BLOCK, BLOCK)

    def step(h, way, g, d):
        owner = lax.rem(at[h] + (1 - 2 * way) * d + n, n)
        values = [chunk(h, c, owner) for c in range(*groups[g])]
        if d < hops_of(n, way, g):
            values = add_arrived(values, h, way, d + 1, g)
        put(h, way, d, g, values)

    def second(h, t, g):
        lo, hi = groups[g]
        there = lax.rem(at[1 - h] + t, n)
        rows, scales = pl.ds(lo * span, (hi - lo) * span), pl.ds(lo, hi - lo)
        to = along(1 - h, t)
        return (remote(c2.at[h, scales], rc2.at[h, t, scales], 5, m2_r.at[h, g], to),
                remote(s2.at[h, there, rows], r2.at[h, t, rows], 3, m2_r.at[h, g], to))

    def own_step(h, g):
        lo, hi = groups[g]
        values = [chunk(h, c, at[h]) for c in range(lo, hi)]
        for way in (0, 1):
            if hops_of(n, way, g) > 0:
                values = add_arrived(values, h, way, 1, g)
        for j, value in enumerate(values):
            fin[h, lo + j] = value
            q, scale = quantize(value)
            for o in range(n):
                s2[h, o, (lo + j) * span:(lo + j + 1) * span, :] = q[o * span:(o + 1) * span]
            c2[h, lo + j:lo + j + 1, :] = scale
        for t in sorted(range(1, n), key=lambda t: -min(t, n - t)):
            for copy in second(h, t, g):
                copy.start()

    def finish(h, g):
        lo, hi = groups[g]
        mine = pl.ds(pl.multiple_of(at[1 - h] * span, span), span)
        values = [fin[h, c, mine, :] for c in range(lo, hi)]
        if n > 1:
            both = part.at[pl.ds(0, n - 1), 0, pl.ds(0, (hi - lo) * (span // 2 + 1))]
            remote(both, both, 3, m2_r.at[h, g], along(1 - h, 1)).wait_recv()
        for t in range(1, n):
            for j in range(hi - lo):
                rows = slice((lo + j) * span, (lo + j + 1) * span)
                values[j] = values[j] + widen(r2[h, t, rows, :], rc2[h, t, lo + j:lo + j + 1, :])
        for j in range(hi - lo):
            out[h * per_half + lo + j] = values[j] * factor

    finishing = []
    for op in order_of(n, groups):
        for h in (0, 1):
            if len(op) == 1:
                products(h, *op)
            elif len(op) == 3:
                step(h, *op)
            else:
                own_step(h, op[0])
                finishing.append((h, op[0]))
    for h, g in finishing:
        finish(h, g)

    def sent(ref, i):
        pltpu.make_async_remote_copy(
            src_ref=ref, dst_ref=ref, send_sem=send_sem.at[i], recv_sem=sib_r.at[0],
            device_id={"dp": dp, "mp": sibling}, device_id_type=MESH).wait_send()

    if nx > 1:
        sent(feat.at[pl.ds(0, 3 * nb)], 0)
    sent(everything, 1)
    if n > 1:
        sent(sn, 2)
        sent(cn, 4)
        sent(s2.at[:, pl.ds(1, n - 1)], 3)
        sent(rc2.at[:, pl.ds(1, n - 1), pl.ds(0, per_half)], 5)


def shards(n, nx, groups, activations, out_grad, row_blocks, doc_lengths):
    slots = activations.shape[0]
    nb = activations.shape[1] // BLOCK
    columns, knz = row_blocks.shape
    per_half = columns // 2
    factor = 1.0 / math.sqrt(slots * n * n)
    cfg = (n, nx, nb, knz, per_half, groups, factor)
    ng = len(groups)
    span = BLOCK // n
    dma = pltpu.SemaphoreType.DMA
    anywhere = pl.BlockSpec(memory_space=pl.ANY)
    chains = [(hi - lo, hops_of(n, way, g)) for g, (lo, hi) in enumerate(groups) for way in (0, 1) for h in (0, 1)]
    messages = max(1, sum(hops for _, hops in chains))
    blocks = max(1, sum(hops * wide for wide, hops in chains))
    return pl.pallas_call(
        functools.partial(kernel, cfg),
        out_shape=jax.ShapeDtypeStruct((columns, span * knz // n, BLOCK), jnp.float32),
        in_specs=[anywhere] * 4,
        out_specs=pl.BlockSpec(memory_space=pltpu.VMEM),
        scratch_shapes=[
            pltpu.VMEM(activations.shape, jnp.bfloat16),
            pltpu.VMEM(out_grad.shape, jnp.bfloat16),
            pltpu.SMEM(row_blocks.shape[::-1], jnp.int32),
            pltpu.SMEM(doc_lengths.shape, jnp.int32),
            pltpu.VMEM((nb * nx * CORES, BLOCK, slots), jnp.bfloat16),
            pltpu.VMEM((columns, slots, BLOCK), jnp.bfloat16),
            pltpu.VMEM((columns, knz, BLOCK, BLOCK), jnp.float32),
            pltpu.VMEM((blocks * BLOCK, BLOCK), jnp.int16),
            pltpu.VMEM((blocks * BLOCK, BLOCK), jnp.int16),
            pltpu.VMEM((blocks, BLOCK), jnp.float32),
            pltpu.VMEM((blocks, BLOCK), jnp.float32),
            pltpu.VMEM((2, n, per_half * span, BLOCK), jnp.int16),
            pltpu.VMEM((2, n, per_half * span, BLOCK), jnp.int16),
            pltpu.VMEM((2, 8, BLOCK), jnp.float32),
            pltpu.VMEM((2, n, 8, BLOCK), jnp.float32),
            pltpu.VMEM((2, per_half, BLOCK, BLOCK), jnp.float32),
            dma((4,)),
            dma((2, nb + nb // 2)),
            dma((1,)),
            dma((messages,)),
            dma((2, ng)),
            dma((6,)),
        ],
        compiler_params=pltpu.CompilerParams(
            collective_id=0, has_side_effects=True, vmem_limit_bytes=40 * 2**20),
    )(*(pltpu.with_memory_space_constraint(a, pltpu.HBM) for a in (activations, out_grad, row_blocks.T, doc_lengths)))


def solution(mesh):
    n = math.isqrt(mesh.shape["dp"])
    body = functools.partial(shards, n, mesh.shape["mp"] // CORES, GROUPS)
    in_specs = (P("dp", "mp"), P("dp", "mp"), P("mp", None), P("dp", None))
    return jax.shard_map(body, mesh=mesh, in_specs=in_specs, out_specs=P("mp", "dp", None), check_vma=False)
```

```python
import functools
import math

import jax
import jax.numpy as jnp
from jax import lax
from jax.experimental import pallas as pl
from jax.experimental.pallas import tpu as pltpu
from jax.sharding import PartitionSpec as P

BLOCK = 128
CORES = 2
TOP = 32700.0
TINY = 1e-33
LEAD = 3
ORDER = (
    ("near", 0), ("near", 1), ("near", 2), ("far", 0), ("near", 3), ("unit", 0), ("far", 1), ("sum", 0, 0, 0, 4),
    ("sum", 1, 0, 0, 4), ("near", 4), ("sum", 1, 1, 1, 4), ("far", 2), ("sum", 0, 1, 0, 3), ("sum", 1, 0, 2, 4),
    ("unit", 1), ("near", 5), ("unit", 2), ("far", 3), ("sum", 0, 1, 1, 4), ("sum", 1, 0, 1, 3), ("sum", 0, 0, 1, 3),
    ("near", 6), ("sum", 1, 1, 0, 3), ("unit", 3), ("far", 4), ("sum", 0, 0, 0, 3), ("near", 7), ("sum", 0, 1, 0, 2),
    ("sum", 1, 1, 3, 4), ("sum", 1, 0, 0, 3), ("far", 5), ("unit", 4), ("sum", 0, 0, 2, 4), ("unit", 5), ("far", 6),
    ("sum", 1, 1, 1, 3), ("sum", 1, 0, 2, 3), ("sum", 0, 1, 1, 3), ("sum", 0, 0, 1, 2), ("far", 7), ("unit", 6),
    ("sum", 0, 1, 3, 4), ("sum", 0, 0, 0, 2), ("unit", 7), ("sum", 1, 0, 0, 2), ("sum", 0, 1, 2, 3),
    ("sum", 1, 0, 1, 2), ("sum", 1, 1, 0, 2), ("sum", 0, 0, 4, 4), ("sum", 1, 1, 4, 3), ("sum", 0, 0, 2, 3),
    ("sum", 0, 1, 4, 3), ("sum", 1, 1, 2, 3), ("sum", 1, 0, 4, 4), ("sum", 0, 1, 0, 1), ("sum", 1, 0, 2, 2),
    ("sum", 0, 0, 3, 3), ("sum", 0, 1, 1, 2), ("sum", 1, 1, 1, 2), ("sum", 1, 0, 3, 3), ("sum", 0, 0, 0, 1),
    ("sum", 0, 1, 3, 3), ("sum", 1, 1, 3, 3), ("sum", 0, 0, 1, 1), ("sum", 1, 0, 0, 1), ("sum", 0, 1, 2, 2),
    ("sum", 1, 0, 1, 1), ("sum", 0, 0, 2, 2), ("sum", 1, 1, 0, 1), ("sum", 1, 1, 2, 2), ("sum", 0, 1, 4, 2),
    ("sum", 1, 0, 4, 3), ("sum", 0, 0, 4, 3), ("sum", 0, 1, 1, 1), ("sum", 1, 1, 1, 1), ("own", 0, 0),
    ("sum", 0, 0, 3, 2), ("sum", 0, 1, 3, 2), ("sum", 1, 1, 3, 2), ("sum", 1, 0, 3, 2), ("own", 1, 0),
    ("sum", 1, 0, 2, 1), ("sum", 0, 0, 2, 1), ("sum", 1, 1, 4, 2), ("sum", 1, 1, 2, 1), ("sum", 0, 1, 2, 1),
    ("sum", 0, 0, 4, 2), ("sum", 1, 0, 4, 2), ("own", 0, 1), ("own", 1, 1), ("sum", 0, 0, 3, 1), ("sum", 1, 0, 3, 1),
    ("sum", 1, 1, 3, 1), ("sum", 0, 1, 3, 1), ("sum", 1, 1, 4, 1), ("sum", 0, 1, 4, 1), ("sum", 0, 0, 4, 1),
    ("sum", 1, 0, 4, 1), ("own", 1, 2), ("own", 0, 2), ("own", 1, 3), ("own", 0, 3), ("own", 1, 4), ("own", 0, 4),
)
MESH = pl.DeviceIdType.MESH


def quantize(x):
    peak = jnp.maximum(jnp.max(jnp.abs(x), axis=0, keepdims=True), TINY)
    return jnp.round(x * (TOP / peak)).astype(jnp.int32).astype(jnp.int16), peak * (1.0 / TOP)


def widen(q, scale):
    return q.astype(jnp.int32).astype(jnp.float32) * scale


def offsets_of(n):
    return sorted(range(n), key=lambda o: (-min(o, n - o), o))


def groups_of(n):
    return [[o for o in offsets_of(n) if min(o, n - o) == d] for d in range(n // 2, -1, -1)]


def hops_of(n, way, g):
    return n // 2 if way == g % 2 else n - 1 - n // 2


def order_of(n):
    if n == 8:
        return ORDER
    order = []
    for j in range(n):
        order += [("near", j), ("far", j), ("unit", j)]
    groups = range(len(groups_of(n)))
    for r in range(n // 2):
        for g in groups:
            for h in (0, 1):
                order += [("sum", h, way, g, hops_of(n, way, g) - r)
                          for way in (g % 2, 1 - g % 2) if hops_of(n, way, g) > r]
    return order + [("own", h, g) for g in groups for h in (0, 1)]


def kernel(cfg, act_hbm, grad_hbm, rb_hbm, docs_hbm, out, act, grad, rb, docs, turn, gm, unit, gauge, sn, rn, cn, rcn,
           s2, r2, c2, rc2, in_sem, x_r, sib_r, m_r, m2_r, send_sem, *feats):
    n, nx, nb, knz, per_half, factor = cfg
    slots = act.shape[0]
    span = BLOCK // n
    high = per_half * span
    offsets, groups = offsets_of(n), groups_of(n)
    place = {o: j for j, o in enumerate(offsets)}
    dp = lax.axis_index("dp")
    mp = lax.axis_index("mp")
    at = (dp // n, lax.rem(dp, n))
    x, core = mp // CORES, lax.rem(mp, CORES)
    sibling = x * CORES + (1 - core)

    def along(axis, step):
        there = lax.rem(at[axis] + step + n, n)
        if axis == 0:
            return {"dp": there * n + at[1], "mp": mp}
        return {"dp": at[0] * n + there, "mp": mp}

    def x_device(step):
        return lax.rem(x + step + nx, nx) * CORES + core

    peers = [{"dp": dp, "mp": sibling}]
    if nx > 1:
        peers += [{"dp": dp, "mp": x_device(1)}, {"dp": dp, "mp": x_device(-1)}]
    if n > 1:
        peers += [along(axis, step) for axis in (0, 1) for step in sorted({1, n - 1, 2 % n, (n - 2) % n} - {0})]
    barrier = pltpu.get_barrier_semaphore()
    for peer in peers:
        pl.semaphore_signal(barrier, inc=1, device_id=peer, device_id_type=MESH)

    loads = [pltpu.make_async_copy(a, b, in_sem.at[i])
             for i, (a, b) in enumerate(((act_hbm, act), (docs_hbm, docs), (rb_hbm, rb), (grad_hbm, grad)))]
    for load in loads:
        load.start()
    loads[0].wait()
    for b in range(nb):
        turn[b] = act[:, b * BLOCK:(b + 1) * BLOCK].T

    def cut(j):
        rows = pl.ds(pl.multiple_of(lax.rem(at[1] + offsets[j], n) * span, span), span)
        for b in range(nb):
            feats[j][mp * nb + b] = turn[b, rows, :]

    for j in range(n):
        cut(j)
    pl.semaphore_wait(barrier, len(peers))

    def remote(src, dst, send, recv, to):
        return pltpu.make_async_remote_copy(
            src_ref=src, dst_ref=dst, send_sem=send_sem.at[send], recv_sem=recv, device_id=to, device_id_type=MESH)

    def push(j, first, size, to, send, recv):
        piece = feats[j].at[pl.ds(first, size)]
        return remote(piece, piece, send, recv, {"dp": dp, "mp": to})

    def share(j, first, size):
        push(j, first, size, sibling, 1, sib_r.at[j]).start()

    half = nb // 2
    if nx > 1:
        right, left, far = x_device(1), x_device(-1), x_device(2)

    def give(j):
        if nx > 1:
            push(j, mp * nb, nb, right, 0, x_r.at[0, j]).start()
            push(j, mp * nb, nb, left, 0, x_r.at[1, j]).start()
        share(j, mp * nb, nb)

    for j in range(min(LEAD, n)):
        give(j)

    for load in loads[1:]:
        load.wait()
    live = docs[0, 0]
    for d in range(1, docs.shape[1]):
        live = live + docs[0, d]
    keep = lax.broadcasted_iota(jnp.int32, (slots, BLOCK), 0) < live
    for c in range(2 * per_half):
        tile = grad[:, c * BLOCK:(c + 1) * BLOCK]
        gm[c] = jnp.where(keep, tile, jnp.zeros_like(tile))

    def near(j):
        if nx > 1:
            push(j, left * nb, nb, right, 0, x_r.at[0, j]).wait_recv()
            push(j, left * nb, half, right, 0, x_r.at[2, j]).start()
            push(j, right * nb, nb, left, 0, x_r.at[1, j]).wait_recv()
            push(j, right * nb + half, half, left, 0, x_r.at[3, j]).start()
        if j + LEAD < n:
            give(j + LEAD)
        if nx > 1:
            share(j, left * nb, nb)
            share(j, right * nb, nb)

    def from_far(j):
        if nx > 1:
            push(j, far * nb, half, right, 0, x_r.at[2, j]).wait_recv()
            share(j, far * nb, half)
            push(j, far * nb + half, half, left, 0, x_r.at[3, j]).wait_recv()
            share(j, far * nb + half, half)

    def products(j):
        push(j, 0, nb * nx, sibling, 1, sib_r.at[j]).wait_recv()
        for c in range(2 * per_half):
            lhs = jnp.concatenate([feats[j][rb[k, c]] for k in range(knz)], axis=0)
            sums = jnp.dot(lhs, gm[c], preferred_element_type=jnp.float32)
            unit[j, :, c] = sums.reshape(knz, span, BLOCK)

    def chunk(h, step, o):
        to_y, to_z = (step, o) if h == 0 else (o, step)
        k = lax.rem(at[0] + to_y + n, n)
        return unit[place[to_z % n], k, h * per_half:(h + 1) * per_half].reshape(high, BLOCK)

    plan, count = {}, 0
    for way in (0, 1):
        for g, group in enumerate(groups):
            for d in range(1, hops_of(n, way, g) + 1):
                for h in (0, 1):
                    plan[h, way, d, g] = (len(plan), count)
                    count += len(group)

    def message(h, way, d, g):
        index, first = plan[h, way, d, g]
        size = len(groups[g])
        to = along(h, 1 - 2 * way)
        rows, scales = pl.ds(first * high, size * high), pl.ds(first, size)
        return (remote(cn.at[scales], rcn.at[scales], 4, m_r.at[index], to),
                remote(sn.at[rows], rn.at[rows], 2, m_r.at[index], to))

    def add_arrived(values, h, way, d, g):
        index, first = plan[h, way, d, g]
        both = gauge.at[pl.ds(0, len(values))]
        remote(both, both, 2, m_r.at[index], along(h, 1 - 2 * way)).wait_recv()
        return [v + widen(rn[(first + i) * high:(first + i + 1) * high, :], rcn[first + i:first + i + 1, :])
                for i, v in enumerate(values)]

    def step(h, way, g, d):
        values = [chunk(h, (1 - 2 * way) * d, o) for o in groups[g]]
        if d < hops_of(n, way, g):
            values = add_arrived(values, h, way, d + 1, g)
        first = plan[h, way, d, g][1]
        for i, value in enumerate(values):
            q, scale = quantize(value)
            sn[(first + i) * high:(first + i + 1) * high, :] = q
            cn[first + i:first + i + 1, :] = scale
        for copy in message(h, way, d, g):
            copy.start()

    def way_of(h, o):
        return 0 if o < n - o or (o == n - o and h == 0) else 1

    def target(h, o):
        hop = min(2, o, n - o)
        return ((o - hop) % n, hop) if way_of(h, o) == 0 else ((o + hop) % n, -hop)

    def second(h, o):
        to = along(1 - h, target(h, o)[1])
        row = pl.ds(h * n + o, 1)
        return (remote(c2.at[row], rc2.at[row], 5, m2_r.at[h, o], to),
                remote(s2.at[h, o], r2.at[h, o], 3, m2_r.at[h, o], to))

    def add_second(value, h, o):
        both = gauge.at[pl.ds(0, 1)]
        remote(both, both, 3, m2_r.at[h, o], along(1 - h, 1)).wait_recv()
        return value + widen(r2[h, o], rc2[h * n + o:h * n + o + 1, :])

    def own_step(h, g):
        values = [chunk(h, 0, o) for o in groups[g]]
        for way in (0, 1):
            if hops_of(n, way, g) > 0:
                values = add_arrived(values, h, way, 1, g)
        for value, o in zip(values, groups[g]):
            for before in range(1, n):
                if target(h, before)[0] == o:
                    value = add_second(value, h, before)
            if o == 0:
                out[h * per_half:(h + 1) * per_half] = (value * factor).reshape(per_half, span, BLOCK)
            else:
                q, scale = quantize(value)
                s2[h, o] = q
                c2[h * n + o:h * n + o + 1, :] = scale
                for copy in second(h, o):
                    copy.start()

    run = {"near": near, "far": from_far, "unit": products, "sum": step, "own": own_step}
    for op in order_of(n):
        run[op[0]](*op[1:])

    def sent(ref, i):
        remote(ref, ref, i, sib_r.at[0], {"dp": dp, "mp": sibling}).wait_send()

    for j in range(n):
        if nx > 1:
            sent(feats[j].at[pl.ds(0, 3 * nb)], 0)
        sent(feats[j].at[pl.ds(0, nb * nx)], 1)
    if n > 1:
        sent(sn, 2)
        sent(cn, 4)
        sent(s2.at[:, pl.ds(1, n - 1)], 3)
        sent(rc2.at[pl.ds(0, 2 * (n - 1))], 5)


def shards(n, nx, activations, out_grad, row_blocks, doc_lengths):
    slots = activations.shape[0]
    nb = activations.shape[1] // BLOCK
    columns, knz = row_blocks.shape
    per_half = columns // 2
    factor = 1.0 / math.sqrt(slots * n * n)
    span = BLOCK // n
    high = per_half * span
    sizes = [(len(group), hops_of(n, way, g)) for g, group in enumerate(groups_of(n)) for way in (0, 1) for h in (0, 1)]
    messages = max(1, sum(hops for _, hops in sizes))
    count = max(1, sum(hops * size for size, hops in sizes))
    dma = pltpu.SemaphoreType.DMA
    operands = (activations, out_grad, row_blocks.T, doc_lengths)
    return pl.pallas_call(
        functools.partial(kernel, (n, nx, nb, knz, per_half, factor)),
        out_shape=jax.ShapeDtypeStruct((columns, span * knz // n, BLOCK), jnp.float32),
        in_specs=[pl.BlockSpec(memory_space=pl.ANY)] * 4,
        out_specs=pl.BlockSpec(memory_space=pltpu.VMEM),
        scratch_shapes=[
            pltpu.VMEM(activations.shape, jnp.bfloat16),
            pltpu.VMEM(out_grad.shape, jnp.bfloat16),
            pltpu.SMEM(row_blocks.shape[::-1], jnp.int32),
            pltpu.SMEM(doc_lengths.shape, jnp.int32),
            pltpu.VMEM((nb, BLOCK, slots), jnp.bfloat16),
            pltpu.VMEM((columns, slots, BLOCK), jnp.bfloat16),
            pltpu.VMEM((n, knz, columns, span, BLOCK), jnp.float32),
            pltpu.VMEM((2, high // 2 + 1, BLOCK), jnp.float32),
            pltpu.VMEM((count * high, BLOCK), jnp.int16),
            pltpu.VMEM((count * high, BLOCK), jnp.int16),
            pltpu.VMEM((count, BLOCK), jnp.float32),
            pltpu.VMEM((count, BLOCK), jnp.float32),
            pltpu.VMEM((2, n, high, BLOCK), jnp.int16),
            pltpu.VMEM((2, n, high, BLOCK), jnp.int16),
            pltpu.VMEM((2 * n, BLOCK), jnp.float32),
            pltpu.VMEM((2 * n, BLOCK), jnp.float32),
            dma((4,)),
            dma((4, n)),
            dma((n,)),
            dma((messages,)),
            dma((2, n)),
            dma((6,)),
        ] + [pltpu.VMEM((nb * nx * CORES, span, slots), jnp.bfloat16)] * n,
        compiler_params=pltpu.CompilerParams(
            collective_id=0, has_side_effects=True, vmem_limit_bytes=40 * 2**20),
    )(*(pltpu.with_memory_space_constraint(a, pltpu.HBM) for a in operands))


def solution(mesh):
    n = math.isqrt(mesh.shape["dp"])
    body = functools.partial(shards, n, mesh.shape["mp"] // CORES)
    in_specs = (P("dp", "mp"), P("dp", "mp"), P("mp", None), P("dp", None))
    return jax.shard_map(body, mesh=mesh, in_specs=in_specs, out_specs=P("mp", "dp", None), check_vma=False)
```

```python
import functools
import math

import jax
import jax.numpy as jnp
from jax import lax
from jax.experimental import pallas as pl
from jax.experimental.pallas import tpu as pltpu
from jax.sharding import PartitionSpec as P

BLOCK = 128
CORES = 2
TOP = 32700.0
TINY = 1e-33
LEAD = 3
DIRECT = 4
FIRST = 6
MESH = pl.DeviceIdType.MESH
ORDER = (
    ("near", 0), ("far", 0), ("near", 1), ("unit", 0, 1), ("unit", 0, 0), ("near", 2), ("far", 1),
    ("sum", 1, 0, 0, 4), ("sum", 1, 0, 4, 4), ("sum", 0, 1, 0, 3), ("sum", 1, 1, 1, 4), ("sum", 1, 0, 2, 4),
    ("unit", 1, 1), ("near", 3), ("far", 2), ("unit", 1, 0), ("sum", 0, 0, 0, 4), ("sum", 1, 1, 3, 4),
    ("sum", 1, 0, 1, 3), ("unit", 2, 1), ("near", 4), ("far", 3), ("unit", 2, 0), ("sum", 0, 1, 1, 4), ("near", 5),
    ("sum", 1, 1, 2, 3), ("sum", 1, 0, 0, 3), ("unit", 3, 1), ("unit", 3, 0), ("sum", 1, 0, 4, 3),
    ("sum", 1, 1, 0, 3), ("near", 6), ("sum", 1, 1, 1, 3), ("sum", 0, 0, 1, 3), ("sum", 1, 0, 3, 3),
    ("sum", 0, 0, 0, 3), ("sum", 0, 1, 0, 2), ("far", 4), ("sum", 1, 1, 4, 3), ("sum", 1, 0, 2, 3), ("near", 7),
    ("unit", 4, 1), ("far", 5), ("unit", 4, 0), ("sum", 0, 0, 2, 4), ("sum", 0, 1, 1, 3), ("far", 6),
    ("sum", 0, 1, 2, 3), ("unit", 5, 1), ("unit", 5, 0), ("unit", 6, 1), ("unit", 6, 0), ("sum", 0, 1, 3, 4),
    ("far", 7), ("sum", 1, 0, 4, 2), ("sum", 1, 1, 0, 2), ("sum", 1, 0, 0, 2), ("sum", 1, 1, 3, 3),
    ("sum", 1, 0, 1, 2), ("unit", 7, 1), ("unit", 7, 0), ("sum", 0, 1, 4, 3), ("sum", 0, 0, 4, 4),
    ("sum", 0, 0, 2, 3), ("sum", 0, 1, 1, 2), ("sum", 1, 1, 1, 2), ("sum", 0, 1, 0, 1), ("sum", 0, 0, 0, 2),
    ("sum", 1, 0, 2, 2), ("sum", 1, 1, 2, 2), ("sum", 0, 1, 2, 2), ("sum", 0, 0, 1, 2), ("sum", 1, 0, 3, 2),
    ("sum", 0, 0, 3, 3), ("sum", 0, 1, 3, 3), ("sum", 1, 1, 0, 1), ("sum", 1, 0, 0, 1), ("sum", 0, 1, 4, 2),
    ("sum", 0, 0, 4, 3), ("sum", 1, 1, 3, 2), ("sum", 1, 0, 4, 1), ("sum", 0, 1, 1, 1), ("sum", 0, 0, 2, 2),
    ("sum", 1, 0, 1, 1), ("sum", 0, 0, 0, 1), ("sum", 1, 1, 1, 1), ("sum", 0, 1, 2, 1), ("sum", 0, 0, 1, 1),
    ("sum", 1, 1, 2, 1), ("sum", 1, 0, 2, 1), ("sum", 0, 1, 3, 2), ("sum", 0, 0, 3, 2), ("sum", 1, 0, 3, 1),
    ("own", 1, 0), ("sum", 0, 0, 4, 2), ("sum", 1, 1, 4, 2), ("sum", 1, 1, 3, 1), ("sum", 0, 1, 4, 1),
    ("sum", 0, 0, 2, 1), ("own", 0, 0), ("own", 1, 1), ("own", 0, 1), ("sum", 0, 1, 3, 1), ("sum", 0, 0, 3, 1),
    ("sum", 0, 0, 4, 1), ("sum", 1, 1, 4, 1), ("own", 1, 2), ("own", 0, 2), ("own", 1, 3), ("own", 0, 3),
    ("own", 1, 4), ("own", 0, 4),
)


def quantize(x):
    peak = jnp.maximum(jnp.max(jnp.abs(x), axis=0, keepdims=True), TINY)
    return jnp.round(x * (TOP / peak)).astype(jnp.int32).astype(jnp.int16), peak * (1.0 / TOP)


def widen(q, scale):
    return q.astype(jnp.int32).astype(jnp.float32) * scale


def offsets_of(n):
    return sorted(range(n), key=lambda o: (-min(o, n - o), o))


def groups_of(n):
    return [[o for o in offsets_of(n) if min(o, n - o) == d] for d in range(n // 2, -1, -1)]


def hops_of(n, way, g):
    return n // 2 if way == g % 2 else n - 1 - n // 2


def order_of(n):
    if n == 8:
        return ORDER
    order = []
    for j in range(n):
        order += [("near", j), ("far", j), ("unit", j, 0), ("unit", j, 1)]
    groups = range(len(groups_of(n)))
    for r in range(n // 2):
        for g in groups:
            for h in (0, 1):
                order += [("sum", h, way, g, hops_of(n, way, g) - r)
                          for way in (g % 2, 1 - g % 2) if hops_of(n, way, g) > r]
    return order + [("own", h, g) for g in groups for h in (0, 1)]


def kernel(cfg, act_hbm, grad_hbm, rb_hbm, docs_hbm, out, act, grad, rb, docs, turn, gm, unit, gauge, sn, rn, cn, rcn,
           s2, r2, c2, rc2, in_sem, x_r, sib_r, m_r, m2_r, send_sem, *feats):
    n, nx, nb, knz, halves, factor = cfg
    slots = act.shape[0]
    span = BLOCK // n
    columns = sum(halves)
    begins = (0, halves[0])
    high = [wide * span for wide in halves]
    offsets, groups = offsets_of(n), groups_of(n)
    place = {o: j for j, o in enumerate(offsets)}
    dp = lax.axis_index("dp")
    mp = lax.axis_index("mp")
    at = (dp // n, lax.rem(dp, n))
    x, core = mp // CORES, lax.rem(mp, CORES)
    sibling = x * CORES + (1 - core)

    def along(axis, step):
        there = lax.rem(at[axis] + step + n, n)
        if axis == 0:
            return {"dp": there * n + at[1], "mp": mp}
        return {"dp": at[0] * n + there, "mp": mp}

    def x_device(step):
        return lax.rem(x + step + nx, nx) * CORES + core

    peers = [{"dp": dp, "mp": sibling}]
    if nx > 1:
        peers += [{"dp": dp, "mp": x_device(step)} for step in (1, 2, 3)]
    if n > 1:
        peers += [along(axis, step) for axis in (0, 1) for step in sorted({1, n - 1, 2 % n, (n - 2) % n} - {0})]
    barrier = pltpu.get_barrier_semaphore()
    for peer in peers:
        pl.semaphore_signal(barrier, inc=1, device_id=peer, device_id_type=MESH)

    loads = [pltpu.make_async_copy(a, b, in_sem.at[i])
             for i, (a, b) in enumerate(((act_hbm, act), (docs_hbm, docs), (rb_hbm, rb), (grad_hbm, grad)))]
    for load in loads:
        load.start()
    loads[0].wait()
    for b in range(nb):
        turn[b] = act[:, b * BLOCK:(b + 1) * BLOCK].T

    def cut(j):
        rows = pl.ds(pl.multiple_of(lax.rem(at[1] + offsets[j], n) * span, span), span)
        for b in range(nb):
            feats[j][mp * nb + b] = turn[b, rows, :]

    for j in range(n):
        cut(j)
    pl.semaphore_wait(barrier, len(peers))

    def remote(src, dst, send, recv, to):
        return pltpu.make_async_remote_copy(
            src_ref=src, dst_ref=dst, send_sem=send_sem.at[send], recv_sem=recv, device_id=to, device_id_type=MESH)

    def push(j, first, size, to, send, recv):
        piece = feats[j].at[pl.ds(first, size)]
        return remote(piece, piece, send, recv, {"dp": dp, "mp": to})

    def share(j, first, size):
        push(j, first, size, sibling, 1, sib_r.at[j]).start()

    half = nb // 2
    if nx > 1:
        right, left, far = x_device(1), x_device(-1), x_device(2)

    def give(j):
        if nx > 1:
            push(j, mp * nb, nb, right, 0, x_r.at[0, j]).start()
            push(j, mp * nb, nb, left, 0, x_r.at[1, j]).start()
            if j < DIRECT:
                push(j, mp * nb, nb, far, 0, x_r.at[2, j]).start()
        share(j, mp * nb, nb)

    for j in range(min(LEAD, n)):
        give(j)

    for load in loads[1:]:
        load.wait()
    live = docs[0, 0]
    for d in range(1, docs.shape[1]):
        live = live + docs[0, d]
    keep = lax.broadcasted_iota(jnp.int32, (slots, BLOCK), 0) < live
    for c in range(columns):
        tile = grad[:, c * BLOCK:(c + 1) * BLOCK]
        gm[c] = jnp.where(keep, tile, jnp.zeros_like(tile))

    def near(j):
        if nx > 1:
            push(j, left * nb, nb, right, 0, x_r.at[0, j]).wait_recv()
            if j >= DIRECT:
                push(j, left * nb, half, right, 0, x_r.at[2, j]).start()
            push(j, right * nb, nb, left, 0, x_r.at[1, j]).wait_recv()
            if j >= DIRECT:
                push(j, right * nb + half, half, left, 0, x_r.at[3, j]).start()
        if j + LEAD < n:
            give(j + LEAD)
        if nx > 1:
            share(j, left * nb, nb)
            share(j, right * nb, nb)

    def from_far(j):
        if nx > 1 and j < DIRECT:
            push(j, far * nb, nb, far, 0, x_r.at[2, j]).wait_recv()
            share(j, far * nb, nb)
        elif nx > 1:
            push(j, far * nb, half, right, 0, x_r.at[2, j]).wait_recv()
            share(j, far * nb, half)
            push(j, far * nb + half, half, left, 0, x_r.at[3, j]).wait_recv()
            share(j, far * nb + half, half)

    complete = set()

    def products(j, h):
        if j not in complete:
            push(j, 0, nb * nx, sibling, 1, sib_r.at[j]).wait_recv()
            complete.add(j)
        for c in range(begins[h], begins[h] + halves[h]):
            lhs = jnp.concatenate([feats[j][rb[k, c]] for k in range(knz)], axis=0)
            sums = jnp.dot(lhs, gm[c], preferred_element_type=jnp.float32)
            unit[j, :, c] = sums.reshape(knz, span, BLOCK)

    def chunk(h, step, o):
        to_y, to_z = (step, o) if h == 0 else (o, step)
        k = lax.rem(at[0] + to_y + n, n)
        return unit[place[to_z % n], k, begins[h]:begins[h] + halves[h]].reshape(high[h], BLOCK)

    plan, count, depth = {}, 0, 0
    for way in (0, 1):
        for g, group in enumerate(groups):
            for d in range(1, hops_of(n, way, g) + 1):
                for h in (0, 1):
                    plan[h, way, d, g] = (len(plan), count, depth)
                    count += len(group)
                    depth += len(group) * high[h]

    def message(h, way, d, g):
        index, first, start = plan[h, way, d, g]
        size = len(groups[g])
        to = along(h, 1 - 2 * way)
        rows, scales = pl.ds(start, size * high[h]), pl.ds(first, size)
        return (remote(cn.at[scales], rcn.at[scales], 4, m_r.at[index], to),
                remote(sn.at[rows], rn.at[rows], 2, m_r.at[index], to))

    def add_arrived(values, h, way, d, g):
        index, first, start = plan[h, way, d, g]
        both = gauge.at[pl.ds(0, len(values)), pl.ds(0, high[h] // 2 + 1)]
        remote(both, both, 2, m_r.at[index], along(h, 1 - 2 * way)).wait_recv()
        return [v + widen(rn[start + i * high[h]:start + (i + 1) * high[h], :], rcn[first + i:first + i + 1, :])
                for i, v in enumerate(values)]

    def step(h, way, g, d):
        values = [chunk(h, (1 - 2 * way) * d, o) for o in groups[g]]
        if d < hops_of(n, way, g):
            values = add_arrived(values, h, way, d + 1, g)
        _, first, start = plan[h, way, d, g]
        for i, value in enumerate(values):
            q, scale = quantize(value)
            sn[start + i * high[h]:start + (i + 1) * high[h], :] = q
            cn[first + i:first + i + 1, :] = scale
        for copy in message(h, way, d, g):
            copy.start()

    def way_of(h, o):
        return 0 if o < n - o or (o == n - o and h == 0) else 1

    def target(h, o):
        hop = min(2, o, n - o)
        return ((o - hop) % n, hop) if way_of(h, o) == 0 else ((o + hop) % n, -hop)

    def second(h, o):
        to = along(1 - h, target(h, o)[1])
        row, rows = pl.ds(h * n + o, 1), pl.ds(begins[h] * span, high[h])
        return (remote(c2.at[row], rc2.at[row], 5, m2_r.at[h, o], to),
                remote(s2.at[o, rows], r2.at[o, rows], 3, m2_r.at[h, o], to))

    def add_second(value, h, o):
        both = gauge.at[pl.ds(0, 1), pl.ds(0, high[h] // 2 + 1)]
        remote(both, both, 3, m2_r.at[h, o], along(1 - h, 1)).wait_recv()
        rows = slice(begins[h] * span, begins[h] * span + high[h])
        return value + widen(r2[o, rows, :], rc2[h * n + o:h * n + o + 1, :])

    def own_step(h, g):
        values = [chunk(h, 0, o) for o in groups[g]]
        for way in (0, 1):
            if hops_of(n, way, g) > 0:
                values = add_arrived(values, h, way, 1, g)
        for value, o in zip(values, groups[g]):
            for before in range(1, n):
                if target(h, before)[0] == o:
                    value = add_second(value, h, before)
            if o == 0:
                out[begins[h]:begins[h] + halves[h]] = (value * factor).reshape(halves[h], span, BLOCK)
            else:
                q, scale = quantize(value)
                s2[o, begins[h] * span:begins[h] * span + high[h], :] = q
                c2[h * n + o:h * n + o + 1, :] = scale
                for copy in second(h, o):
                    copy.start()

    run = {"near": near, "far": from_far, "unit": products, "sum": step, "own": own_step}
    for op in order_of(n):
        run[op[0]](*op[1:])

    def sent(ref, i):
        remote(ref, ref, i, sib_r.at[0], {"dp": dp, "mp": sibling}).wait_send()

    for j in range(n):
        if nx > 1:
            sent(feats[j].at[pl.ds(0, 3 * nb)], 0)
        sent(feats[j].at[pl.ds(0, nb * nx)], 1)
    if n > 1:
        sent(sn, 2)
        sent(cn, 4)
        sent(s2.at[pl.ds(1, n - 1)], 3)
        sent(rc2.at[pl.ds(0, 2 * (n - 1))], 5)


def shards(n, nx, activations, out_grad, row_blocks, doc_lengths):
    slots = activations.shape[0]
    nb = activations.shape[1] // BLOCK
    columns, knz = row_blocks.shape
    first = FIRST if columns == 14 else columns // 2 - 1
    halves = (first, columns - first)
    factor = 1.0 / math.sqrt(slots * n * n)
    span = BLOCK // n
    sizes = [(len(group), hops_of(n, way, g)) for g, group in enumerate(groups_of(n)) for way in (0, 1) for h in (0, 1)]
    messages = max(1, sum(hops for _, hops in sizes))
    count = max(1, sum(hops * size for size, hops in sizes))
    depth = max(16, columns * span * sum(hops * size for size, hops in sizes) // 2)
    dma = pltpu.SemaphoreType.DMA
    operands = (activations, out_grad, row_blocks.T, doc_lengths)
    return pl.pallas_call(
        functools.partial(kernel, (n, nx, nb, knz, halves, factor)),
        out_shape=jax.ShapeDtypeStruct((columns, span * knz // n, BLOCK), jnp.float32),
        in_specs=[pl.BlockSpec(memory_space=pl.ANY)] * 4,
        out_specs=pl.BlockSpec(memory_space=pltpu.VMEM),
        scratch_shapes=[
            pltpu.VMEM(activations.shape, jnp.bfloat16),
            pltpu.VMEM(out_grad.shape, jnp.bfloat16),
            pltpu.SMEM(row_blocks.shape[::-1], jnp.int32),
            pltpu.SMEM(doc_lengths.shape, jnp.int32),
            pltpu.VMEM((nb, BLOCK, slots), jnp.bfloat16),
            pltpu.VMEM((columns, slots, BLOCK), jnp.bfloat16),
            pltpu.VMEM((n, knz, columns, span, BLOCK), jnp.float32),
            pltpu.VMEM((2, max(halves) * span // 2 + 1, BLOCK), jnp.float32),
            pltpu.VMEM((depth, BLOCK), jnp.int16),
            pltpu.VMEM((depth, BLOCK), jnp.int16),
            pltpu.VMEM((count, BLOCK), jnp.float32),
            pltpu.VMEM((count, BLOCK), jnp.float32),
            pltpu.VMEM((n, columns * span, BLOCK), jnp.int16),
            pltpu.VMEM((n, columns * span, BLOCK), jnp.int16),
            pltpu.VMEM((2 * n, BLOCK), jnp.float32),
            pltpu.VMEM((2 * n, BLOCK), jnp.float32),
            dma((4,)),
            dma((4, n)),
            dma((n,)),
            dma((messages,)),
            dma((2, n)),
            dma((6,)),
        ] + [pltpu.VMEM((nb * nx * CORES, span, slots), jnp.bfloat16)] * n,
        compiler_params=pltpu.CompilerParams(
            collective_id=0, has_side_effects=True, vmem_limit_bytes=40 * 2**20),
    )(*(pltpu.with_memory_space_constraint(a, pltpu.HBM) for a in operands))


def solution(mesh):
    n = math.isqrt(mesh.shape["dp"])
    body = functools.partial(shards, n, mesh.shape["mp"] // CORES)
    in_specs = (P("dp", "mp"), P("dp", "mp"), P("mp", None), P("dp", None))
    return jax.shard_map(body, mesh=mesh, in_specs=in_specs, out_specs=P("mp", "dp", None), check_vma=False)
```

```python
import functools
import math

import jax
import jax.numpy as jnp
from jax import lax
from jax.experimental import pallas as pl
from jax.experimental.pallas import tpu as pltpu
from jax.sharding import PartitionSpec as P

BLOCK = 128
CORES = 2
TOP = 32700.0
TINY = 1e-33
PAIRS = True
JUMPS = (0, 1, 2, 2, 2)
FIRST = 6
MESH = pl.DeviceIdType.MESH
ORDER = (
    ("near", 0), ("unit", 0, 1), ("unit", 0, 0), ("near", 1), ("sum", 1, 0, 0, 4), ("sum", 1, 0, 4, 4),
    ("sum", 0, 1, 0, 3), ("sum", 1, 1, 1, 4), ("sum", 1, 0, 2, 4), ("unit", 1, 1), ("near", 2), ("unit", 1, 0),
    ("sum", 0, 0, 0, 4), ("sum", 1, 1, 3, 4), ("sum", 1, 0, 1, 3), ("unit", 2, 1), ("near", 3), ("unit", 2, 0),
    ("sum", 0, 1, 1, 4), ("sum", 1, 1, 2, 3), ("sum", 1, 0, 0, 3), ("unit", 3, 1), ("unit", 3, 0),
    ("sum", 1, 0, 4, 3), ("sum", 1, 1, 0, 3), ("sum", 1, 1, 1, 3), ("sum", 0, 0, 1, 3), ("sum", 1, 0, 3, 3),
    ("sum", 0, 0, 0, 3), ("sum", 0, 1, 0, 2), ("near", 4), ("sum", 1, 1, 4, 3), ("sum", 1, 0, 2, 3), ("unit", 4, 1),
    ("near", 5), ("unit", 4, 0), ("sum", 0, 0, 2, 4), ("sum", 0, 1, 1, 3), ("near", 6), ("sum", 0, 1, 2, 3),
    ("unit", 5, 1), ("unit", 5, 0), ("unit", 6, 1), ("unit", 6, 0), ("sum", 0, 1, 3, 4), ("near", 7),
    ("sum", 1, 0, 4, 2), ("sum", 1, 1, 0, 2), ("sum", 1, 0, 0, 2), ("sum", 1, 1, 3, 3), ("sum", 1, 0, 1, 2),
    ("unit", 7, 1), ("unit", 7, 0), ("sum", 0, 1, 4, 3), ("sum", 0, 0, 4, 4), ("sum", 0, 0, 2, 3),
    ("sum", 0, 1, 1, 2), ("sum", 1, 1, 1, 2), ("sum", 0, 1, 0, 1), ("sum", 0, 0, 0, 2), ("sum", 1, 0, 2, 2),
    ("sum", 1, 1, 2, 2), ("sum", 0, 1, 2, 2), ("sum", 0, 0, 1, 2), ("sum", 1, 0, 3, 2), ("sum", 0, 0, 3, 3),
    ("sum", 0, 1, 3, 3), ("sum", 1, 1, 0, 1), ("sum", 1, 0, 0, 1), ("sum", 0, 1, 4, 2), ("sum", 0, 0, 4, 3),
    ("sum", 1, 1, 3, 2), ("sum", 1, 0, 4, 1), ("sum", 0, 1, 1, 1), ("sum", 0, 0, 2, 2), ("sum", 1, 0, 1, 1),
    ("sum", 0, 0, 0, 1), ("sum", 1, 1, 1, 1), ("sum", 0, 1, 2, 1), ("sum", 0, 0, 1, 1), ("sum", 1, 1, 2, 1),
    ("sum", 1, 0, 2, 1), ("sum", 0, 1, 3, 2), ("sum", 0, 0, 3, 2), ("sum", 1, 0, 3, 1), ("own", 1, 0),
    ("sum", 0, 0, 4, 2), ("sum", 1, 1, 4, 2), ("sum", 1, 1, 3, 1), ("sum", 0, 1, 4, 1), ("sum", 0, 0, 2, 1),
    ("own", 0, 0), ("own", 1, 1), ("own", 0, 1), ("sum", 0, 1, 3, 1), ("sum", 0, 0, 3, 1), ("sum", 0, 0, 4, 1),
    ("sum", 1, 1, 4, 1), ("own", 1, 2), ("own", 0, 2), ("own", 1, 3), ("own", 0, 3), ("own", 1, 4), ("own", 0, 4),
)


def quantize(x):
    peak = jnp.maximum(jnp.max(jnp.abs(x), axis=0, keepdims=True), TINY)
    return jnp.round(x * (TOP / peak)).astype(jnp.int32).astype(jnp.int16), peak * (1.0 / TOP)


def widen(q, scale):
    return q.astype(jnp.int32).astype(jnp.float32) * scale


def offsets_of(n):
    return sorted(range(n), key=lambda o: (-min(o, n - o), o))


def groups_of(n):
    if not PAIRS:
        return [[o] for o in offsets_of(n)]
    return [[o for o in offsets_of(n) if min(o, n - o) == d] for d in range(n // 2, -1, -1)]


def hops_of(n, way, g):
    return n // 2 if way == g % 2 else n - 1 - n // 2


def order_of(n):
    if n == 8:
        return ORDER
    order = []
    for j in range(n):
        order += [("near", j), ("unit", j, 0), ("unit", j, 1)]
    groups = range(len(groups_of(n)))
    for r in range(n // 2):
        for g in groups:
            for h in (0, 1):
                order += [("sum", h, way, g, hops_of(n, way, g) - r)
                          for way in (g % 2, 1 - g % 2) if hops_of(n, way, g) > r]
    return order + [("own", h, g) for g in groups for h in (0, 1)]


def kernel(cfg, act_hbm, grad_hbm, rb_hbm, docs_hbm, out, act, grad, rb, docs, turn, gm, unit, gauge, sn, rn, cn, rcn,
           s2, r2, c2, rc2, in_sem, x_r, sib_r, m_r, last_r, m2_r, send_sem, *feats):
    n, nx, nb, knz, halves, factor = cfg
    slots = act.shape[0]
    span = BLOCK // n
    columns = sum(halves)
    begins = (0, halves[0])
    high = [wide * span for wide in halves]
    offsets, groups = offsets_of(n), groups_of(n)
    place = {o: j for j, o in enumerate(offsets)}
    dp = lax.axis_index("dp")
    mp = lax.axis_index("mp")
    at = (dp // n, lax.rem(dp, n))
    x, core = mp // CORES, lax.rem(mp, CORES)
    sibling = x * CORES + (1 - core)

    def along(axis, step):
        there = lax.rem(at[axis] + step + n, n)
        if axis == 0:
            return {"dp": there * n + at[1], "mp": mp}
        return {"dp": at[0] * n + there, "mp": mp}

    def x_device(step):
        return lax.rem(x + step + nx, nx) * CORES + core

    peers = [{"dp": dp, "mp": sibling}]
    if nx > 1:
        peers += [{"dp": dp, "mp": x_device(step)} for step in (1, 2, 3)]
    if n > 1:
        peers += [along(axis, step) for axis in (0, 1) for step in sorted({(sign * hop) % n for hop in set(JUMPS) for sign in (1, -1)} - {0})]
    barrier = pltpu.get_barrier_semaphore()
    for peer in peers:
        pl.semaphore_signal(barrier, inc=1, device_id=peer, device_id_type=MESH)

    loads = [pltpu.make_async_copy(a, b, in_sem.at[i])
             for i, (a, b) in enumerate(((act_hbm, act), (docs_hbm, docs), (rb_hbm, rb), (grad_hbm, grad)))]
    for load in loads:
        load.start()
    loads[0].wait()
    for b in range(nb):
        turn[b] = act[:, b * BLOCK:(b + 1) * BLOCK].T

    def cut(j):
        rows = pl.ds(pl.multiple_of(lax.rem(at[1] + offsets[j], n) * span, span), span)
        for b in range(nb):
            feats[j][mp * nb + b] = turn[b, rows, :]

    for j in range(n):
        cut(j)
    pl.semaphore_wait(barrier, len(peers))

    def remote(src, dst, send, recv, to):
        return pltpu.make_async_remote_copy(
            src_ref=src, dst_ref=dst, send_sem=send_sem.at[send], recv_sem=recv, device_id=to, device_id_type=MESH)

    def push(j, first, size, to, send, recv):
        piece = feats[j].at[pl.ds(first, size)]
        return remote(piece, piece, send, recv, {"dp": dp, "mp": to})

    def share(j, first, size):
        push(j, first, size, sibling, 1, sib_r.at[j]).start()

    others = [x_device(step) for step in (2, 1, 3)] if nx > 1 else []
    for j in range(n):
        for to in others:
            push(j, mp * nb, nb, to, 0, x_r.at[j]).start()
        share(j, mp * nb, nb)

    for load in loads[1:]:
        load.wait()
    live = docs[0, 0]
    for d in range(1, docs.shape[1]):
        live = live + docs[0, d]
    keep = lax.broadcasted_iota(jnp.int32, (slots, BLOCK), 0) < live
    for c in range(columns):
        tile = grad[:, c * BLOCK:(c + 1) * BLOCK]
        gm[c] = jnp.where(keep, tile, jnp.zeros_like(tile))

    def near(j):
        if nx > 1:
            push(j, 0, 3 * nb, sibling, 0, x_r.at[j]).wait_recv()
        for device in others:
            share(j, device * nb, nb)

    complete = set()

    def products(j, h):
        if j not in complete:
            push(j, 0, nb * nx, sibling, 1, sib_r.at[j]).wait_recv()
            complete.add(j)
        for c in range(begins[h], begins[h] + halves[h]):
            lhs = jnp.concatenate([feats[j][rb[k, c]] for k in range(knz)], axis=0)
            sums = jnp.dot(lhs, gm[c], preferred_element_type=jnp.float32)
            unit[j, :, c] = sums.reshape(knz, span, BLOCK)

    def chunk(h, step, o):
        to_y, to_z = (step, o) if h == 0 else (o, step)
        k = lax.rem(at[0] + to_y + n, n)
        return unit[place[to_z % n], k, begins[h]:begins[h] + halves[h]].reshape(high[h], BLOCK)

    plan, early, count, depth = {}, 0, 0, 0
    for way in (0, 1):
        for g, group in enumerate(groups):
            for d in range(1, hops_of(n, way, g) + 1):
                for h in (0, 1):
                    recv = last_r.at[h, g] if d == 1 else m_r.at[early]
                    early += d > 1
                    plan[h, way, d, g] = (recv, count, depth)
                    count += len(group)
                    depth += len(group) * high[h]

    def message(h, way, d, g):
        recv, first, start = plan[h, way, d, g]
        size = len(groups[g])
        to = along(h, 1 - 2 * way)
        rows, scales = pl.ds(start, size * high[h]), pl.ds(first, size)
        return (remote(cn.at[scales], rcn.at[scales], 4, recv, to),
                remote(sn.at[rows], rn.at[rows], 2, recv, to))

    def arrived(slots, h, send, recv):
        both = gauge.at[pl.ds(0, slots), pl.ds(0, high[h] // 2 + 1)]
        remote(both, both, send, recv, along(h, 1)).wait_recv()

    def add(values, h, way, d, g):
        _, first, start = plan[h, way, d, g]
        return [v + widen(rn[start + i * high[h]:start + (i + 1) * high[h], :], rcn[first + i:first + i + 1, :])
                for i, v in enumerate(values)]

    def step(h, way, g, d):
        values = [chunk(h, (1 - 2 * way) * d, o) for o in groups[g]]
        if d < hops_of(n, way, g):
            arrived(len(values), h, 2, plan[h, way, d + 1, g][0])
            values = add(values, h, way, d + 1, g)
        _, first, start = plan[h, way, d, g]
        for i, value in enumerate(values):
            q, scale = quantize(value)
            sn[start + i * high[h]:start + (i + 1) * high[h], :] = q
            cn[first + i:first + i + 1, :] = scale
        for copy in message(h, way, d, g):
            copy.start()

    def way_of(h, o):
        return 0 if o < n - o or (o == n - o and h == 0) else 1

    def target(h, o):
        hop = JUMPS[min(o, n - o)]
        return ((o - hop) % n, hop) if way_of(h, o) == 0 else ((o + hop) % n, -hop)

    def second(h, o):
        goals = sorted({target(h, b)[0] for b in range(1, n)})
        goal = m2_r.at[h, goals.index(target(h, o)[0])]
        to = along(1 - h, target(h, o)[1])
        row, rows = pl.ds(h * n + o, 1), pl.ds(begins[h] * span, high[h])
        return (remote(c2.at[row], rc2.at[row], 5, goal, to),
                remote(s2.at[o, rows], r2.at[o, rows], 3, goal, to))

    def own_step(h, g):
        values = [chunk(h, 0, o) for o in groups[g]]
        ways = [way for way in (0, 1) if hops_of(n, way, g) > 0]
        if ways:
            arrived(len(ways) * len(values), h, 2, last_r.at[h, g])
        for way in ways:
            values = add(values, h, way, 1, g)
        goals = sorted({target(h, b)[0] for b in range(1, n)})
        for value, o in zip(values, groups[g]):
            sources = [b for b in range(1, n) if target(h, b)[0] == o]
            if sources:
                arrived(len(sources), h, 3, m2_r.at[h, goals.index(o)])
            for b in sources:
                rows = slice(begins[h] * span, begins[h] * span + high[h])
                value = value + widen(r2[b, rows, :], rc2[h * n + b:h * n + b + 1, :])
            if o == 0:
                out[begins[h]:begins[h] + halves[h]] = (value * factor).reshape(halves[h], span, BLOCK)
            else:
                q, scale = quantize(value)
                s2[o, begins[h] * span:begins[h] * span + high[h], :] = q
                c2[h * n + o:h * n + o + 1, :] = scale
                for copy in second(h, o):
                    copy.start()

    run = {"near": near, "unit": products, "sum": step, "own": own_step}
    for op in order_of(n):
        run[op[0]](*op[1:])

    def sent(ref, i):
        remote(ref, ref, i, sib_r.at[0], {"dp": dp, "mp": sibling}).wait_send()

    for j in range(n):
        if nx > 1:
            sent(feats[j].at[pl.ds(0, 3 * nb)], 0)
        sent(feats[j].at[pl.ds(0, nb * nx)], 1)
    if n > 1:
        sent(sn, 2)
        sent(cn, 4)
        sent(s2.at[pl.ds(1, n - 1)], 3)
        sent(rc2.at[pl.ds(0, 2 * (n - 1))], 5)


def shards(n, nx, activations, out_grad, row_blocks, doc_lengths):
    slots = activations.shape[0]
    nb = activations.shape[1] // BLOCK
    columns, knz = row_blocks.shape
    first = FIRST if columns == 14 else columns // 2 - 1
    halves = (first, columns - first)
    factor = 1.0 / math.sqrt(slots * n * n)
    span = BLOCK // n
    sizes = [(len(group), hops_of(n, way, g)) for g, group in enumerate(groups_of(n)) for way in (0, 1) for h in (0, 1)]
    messages = max(1, sum(max(0, hops - 1) for _, hops in sizes))
    count = max(1, sum(hops * size for size, hops in sizes))
    depth = max(16, columns * span * sum(hops * size for size, hops in sizes) // 2)
    dma = pltpu.SemaphoreType.DMA
    operands = (activations, out_grad, row_blocks.T, doc_lengths)
    return pl.pallas_call(
        functools.partial(kernel, (n, nx, nb, knz, halves, factor)),
        out_shape=jax.ShapeDtypeStruct((columns, span * knz // n, BLOCK), jnp.float32),
        in_specs=[pl.BlockSpec(memory_space=pl.ANY)] * 4,
        out_specs=pl.BlockSpec(memory_space=pltpu.VMEM),
        scratch_shapes=[
            pltpu.VMEM(activations.shape, jnp.bfloat16),
            pltpu.VMEM(out_grad.shape, jnp.bfloat16),
            pltpu.SMEM(row_blocks.shape[::-1], jnp.int32),
            pltpu.SMEM(doc_lengths.shape, jnp.int32),
            pltpu.VMEM((nb, BLOCK, slots), jnp.bfloat16),
            pltpu.VMEM((columns, slots, BLOCK), jnp.bfloat16),
            pltpu.VMEM((n, knz, columns, span, BLOCK), jnp.float32),
            pltpu.VMEM((4, max(halves) * span // 2 + 1, BLOCK), jnp.float32),
            pltpu.VMEM((depth, BLOCK), jnp.int16),
            pltpu.VMEM((depth, BLOCK), jnp.int16),
            pltpu.VMEM((count, BLOCK), jnp.float32),
            pltpu.VMEM((count, BLOCK), jnp.float32),
            pltpu.VMEM((n, columns * span, BLOCK), jnp.int16),
            pltpu.VMEM((n, columns * span, BLOCK), jnp.int16),
            pltpu.VMEM((2 * n, BLOCK), jnp.float32),
            pltpu.VMEM((2 * n, BLOCK), jnp.float32),
            dma((4,)),
            dma((n,)),
            dma((n,)),
            dma((messages,)),
            dma((2, len(groups_of(n)))),
            dma((2, min(4, n))),
            dma((6,)),
        ] + [pltpu.VMEM((nb * nx * CORES, span, slots), jnp.bfloat16)] * n,
        compiler_params=pltpu.CompilerParams(
            collective_id=0, has_side_effects=True, vmem_limit_bytes=40 * 2**20),
    )(*(pltpu.with_memory_space_constraint(a, pltpu.HBM) for a in operands))


def solution(mesh):
    n = math.isqrt(mesh.shape["dp"])
    body = functools.partial(shards, n, mesh.shape["mp"] // CORES)
    in_specs = (P("dp", "mp"), P("dp", "mp"), P("mp", None), P("dp", None))
    return jax.shard_map(body, mesh=mesh, in_specs=in_specs, out_specs=P("mp", "dp", None), check_vma=False)
```

```python
import functools
import math

import jax
import jax.numpy as jnp
from jax import lax
from jax.experimental import pallas as pl
from jax.experimental.pallas import tpu as pltpu
from jax.sharding import PartitionSpec as P

BLOCK = 128
CORES = 2
TOP = 32700.0
TINY = 1e-33
PAIRS = True
JUMPS = (0, 1, 2, 2, 2)
FIRST = 6
MESH = pl.DeviceIdType.MESH
ORDER = (
    ("near", 0), ("unit", 0, 1), ("unit", 0, 0), ("near", 1), ("sum", 1, 0, 0, 4), ("sum", 1, 0, 4, 4),
    ("sum", 0, 1, 0, 3), ("sum", 1, 1, 1, 4), ("sum", 1, 0, 2, 4), ("unit", 1, 1), ("near", 2), ("unit", 1, 0),
    ("sum", 0, 0, 0, 4), ("sum", 1, 1, 3, 4), ("sum", 1, 0, 1, 3), ("unit", 2, 1), ("near", 3), ("unit", 2, 0),
    ("sum", 0, 1, 1, 4), ("sum", 1, 1, 2, 3), ("sum", 1, 0, 0, 3), ("unit", 3, 1), ("unit", 3, 0),
    ("sum", 1, 0, 4, 3), ("sum", 1, 1, 0, 3), ("sum", 1, 1, 1, 3), ("sum", 0, 0, 1, 3), ("sum", 1, 0, 3, 3),
    ("sum", 0, 0, 0, 3), ("sum", 0, 1, 0, 2), ("near", 4), ("sum", 1, 1, 4, 3), ("sum", 1, 0, 2, 3), ("unit", 4, 1),
    ("near", 5), ("unit", 4, 0), ("sum", 0, 0, 2, 4), ("sum", 0, 1, 1, 3), ("near", 6), ("sum", 0, 1, 2, 3),
    ("unit", 5, 1), ("unit", 5, 0), ("unit", 6, 1), ("unit", 6, 0), ("sum", 0, 1, 3, 4), ("near", 7),
    ("sum", 1, 0, 4, 2), ("sum", 1, 1, 0, 2), ("sum", 1, 0, 0, 2), ("sum", 1, 1, 3, 3), ("sum", 1, 0, 1, 2),
    ("unit", 7, 1), ("unit", 7, 0), ("sum", 0, 1, 4, 3), ("sum", 0, 0, 4, 4), ("sum", 0, 0, 2, 3),
    ("sum", 0, 1, 1, 2), ("sum", 1, 1, 1, 2), ("sum", 0, 1, 0, 1), ("sum", 0, 0, 0, 2), ("sum", 1, 0, 2, 2),
    ("sum", 1, 1, 2, 2), ("sum", 0, 1, 2, 2), ("sum", 0, 0, 1, 2), ("sum", 1, 0, 3, 2), ("sum", 0, 0, 3, 3),
    ("sum", 0, 1, 3, 3), ("sum", 1, 1, 0, 1), ("sum", 1, 0, 0, 1), ("sum", 0, 1, 4, 2), ("sum", 0, 0, 4, 3),
    ("sum", 1, 1, 3, 2), ("sum", 1, 0, 4, 1), ("sum", 0, 1, 1, 1), ("sum", 0, 0, 2, 2), ("sum", 1, 0, 1, 1),
    ("sum", 0, 0, 0, 1), ("sum", 1, 1, 1, 1), ("sum", 0, 1, 2, 1), ("sum", 0, 0, 1, 1), ("sum", 1, 1, 2, 1),
    ("sum", 1, 0, 2, 1), ("sum", 0, 1, 3, 2), ("sum", 0, 0, 3, 2), ("sum", 1, 0, 3, 1), ("own", 1, 0),
    ("sum", 0, 0, 4, 2), ("sum", 1, 1, 4, 2), ("sum", 1, 1, 3, 1), ("sum", 0, 1, 4, 1), ("sum", 0, 0, 2, 1),
    ("own", 0, 0), ("own", 1, 1), ("own", 0, 1), ("sum", 0, 1, 3, 1), ("sum", 0, 0, 3, 1), ("sum", 0, 0, 4, 1),
    ("sum", 1, 1, 4, 1), ("own", 1, 2), ("own", 0, 2), ("own", 1, 3), ("own", 0, 3), ("own", 1, 4), ("own", 0, 4),
)


def quantize(x):
    peak = jnp.maximum(jnp.max(jnp.abs(x), axis=0, keepdims=True), TINY)
    return jnp.round(x * (TOP / peak)).astype(jnp.int32).astype(jnp.int16), peak * (1.0 / TOP)


def widen(q, scale):
    return q.astype(jnp.int32).astype(jnp.float32) * scale


def offsets_of(n):
    return sorted(range(n), key=lambda o: (-min(o, n - o), o))


def groups_of(n):
    if not PAIRS:
        return [[o] for o in offsets_of(n)]
    return [[o for o in offsets_of(n) if min(o, n - o) == d] for d in range(n // 2, -1, -1)]


def hops_of(n, way, g):
    return n // 2 if way == g % 2 else n - 1 - n // 2


def order_of(n):
    if n == 8:
        return ORDER
    order = []
    for j in range(n):
        order += [("near", j), ("unit", j, 0), ("unit", j, 1)]
    groups = range(len(groups_of(n)))
    for r in range(n // 2):
        for g in groups:
            for h in (0, 1):
                order += [("sum", h, way, g, hops_of(n, way, g) - r)
                          for way in (g % 2, 1 - g % 2) if hops_of(n, way, g) > r]
    return order + [("own", h, g) for g in groups for h in (0, 1)]


def kernel(cfg, act_hbm, grad_hbm, rb_hbm, docs_hbm, out, act, grad, rb, docs, spot, turn, gm, unit, gauge, sn, rn, cn, rcn,
           s2, r2, c2, rc2, in_sem, x_r, sib_r, m_r, last_r, m2_r, send_sem, *feats):
    n, nx, nb, knz, halves, factor = cfg
    slots = act.shape[0]
    span = BLOCK // n
    columns = sum(halves)
    begins = (0, halves[0])
    high = [wide * span for wide in halves]
    offsets, groups = offsets_of(n), groups_of(n)
    place = {o: j for j, o in enumerate(offsets)}
    dp = lax.axis_index("dp")
    mp = lax.axis_index("mp")
    at = (dp // n, lax.rem(dp, n))
    x, core = mp // CORES, lax.rem(mp, CORES)
    sibling = x * CORES + (1 - core)

    def along(axis, step):
        there = lax.rem(at[axis] + step + n, n)
        if axis == 0:
            return {"dp": there * n + at[1], "mp": mp}
        return {"dp": at[0] * n + there, "mp": mp}

    def x_device(step):
        return lax.rem(x + step + nx, nx) * CORES + core

    peers = [{"dp": dp, "mp": sibling}]
    if nx > 1:
        peers += [{"dp": dp, "mp": x_device(step)} for step in (1, 2, 3)]
    if n > 1:
        peers += [along(axis, step) for axis in (0, 1) for step in sorted({(sign * hop) % n for hop in set(JUMPS) for sign in (1, -1)} - {0})]
    barrier = pltpu.get_barrier_semaphore()
    for peer in peers:
        pl.semaphore_signal(barrier, inc=1, device_id=peer, device_id_type=MESH)

    loads = [pltpu.make_async_copy(a, b, in_sem.at[i])
             for i, (a, b) in enumerate(((act_hbm, act), (docs_hbm, docs), (rb_hbm, rb), (grad_hbm, grad)))]
    for load in loads:
        load.start()
    loads[0].wait()
    for b in range(nb):
        turn[b] = act[:, b * BLOCK:(b + 1) * BLOCK].T

    def cut(j):
        rows = pl.ds(pl.multiple_of(lax.rem(at[1] + offsets[j], n) * span, span), span)
        for b in range(nb):
            feats[j][b] = turn[b, rows, :]

    for j in range(n):
        cut(j)
    pl.semaphore_wait(barrier, len(peers))

    def remote(src, dst, send, recv, to):
        return pltpu.make_async_remote_copy(
            src_ref=src, dst_ref=dst, send_sem=send_sem.at[send], recv_sem=recv, device_id=to, device_id_type=MESH)

    def push(j, first, size, there, to, send, recv):
        return remote(feats[j].at[pl.ds(first, size)], feats[j].at[pl.ds(there, size)], send, recv, {"dp": dp, "mp": to})

    def share(j, first, size):
        push(j, first, size, nx * nb + first, sibling, 1, sib_r.at[j]).start()

    others = (2, 1, 3) if nx > 1 else ()
    for j in range(n):
        for step in others:
            push(j, 0, nb, (nx - step) * nb, x_device(step), 0, x_r.at[j]).start()
    for j in range(n):
        share(j, 0, nb)

    for load in loads[1:]:
        load.wait()
    live = docs[0, 0]
    for d in range(1, docs.shape[1]):
        live = live + docs[0, d]
    keep = lax.broadcasted_iota(jnp.int32, (slots, BLOCK), 0) < live
    for c in range(columns):
        for k in range(knz):
            owner, block = lax.div(rb[k, c], nb), lax.rem(rb[k, c], nb)
            part = lax.rem(lax.rem(owner, CORES) + core, CORES)
            chip = lax.rem(lax.div(owner, CORES) - x + nx, nx)
            spot[k, c] = (part * nx + chip) * nb + block
        tile = grad[:, c * BLOCK:(c + 1) * BLOCK]
        gm[c] = jnp.where(keep, tile, jnp.zeros_like(tile))

    def near(j):
        if nx > 1:
            push(j, nb, 3 * nb, nb, sibling, 0, x_r.at[j]).wait_recv()
            share(j, nb, 3 * nb)

    complete = set()

    def products(j, h):
        if j not in complete:
            push(j, 0, nb * nx, 0, sibling, 1, sib_r.at[j]).wait_recv()
            complete.add(j)
        for c in range(begins[h], begins[h] + halves[h]):
            lhs = jnp.concatenate([feats[j][spot[k, c]] for k in range(knz)], axis=0)
            sums = jnp.dot(lhs, gm[c], preferred_element_type=jnp.float32)
            unit[j, :, c] = sums.reshape(knz, span, BLOCK)

    def chunk(h, step, o):
        to_y, to_z = (step, o) if h == 0 else (o, step)
        k = lax.rem(at[0] + to_y + n, n)
        return unit[place[to_z % n], k, begins[h]:begins[h] + halves[h]].reshape(high[h], BLOCK)

    plan, early, count, depth = {}, 0, 0, 0
    for way in (0, 1):
        for g, group in enumerate(groups):
            for d in range(1, hops_of(n, way, g) + 1):
                for h in (0, 1):
                    recv = last_r.at[h, g] if d == 1 else m_r.at[early]
                    early += d > 1
                    plan[h, way, d, g] = (recv, count, depth)
                    count += len(group)
                    depth += len(group) * high[h]

    def message(h, way, d, g):
        recv, first, start = plan[h, way, d, g]
        size = len(groups[g])
        to = along(h, 1 - 2 * way)
        rows, scales = pl.ds(start, size * high[h]), pl.ds(first, size)
        return (remote(cn.at[scales], rcn.at[scales], 4, recv, to),
                remote(sn.at[rows], rn.at[rows], 2, recv, to))

    def arrived(slots, h, send, recv):
        both = gauge.at[pl.ds(0, slots), pl.ds(0, high[h] // 2 + 1)]
        remote(both, both, send, recv, along(h, 1)).wait_recv()

    def add(values, h, way, d, g):
        _, first, start = plan[h, way, d, g]
        return [v + widen(rn[start + i * high[h]:start + (i + 1) * high[h], :], rcn[first + i:first + i + 1, :])
                for i, v in enumerate(values)]

    def step(h, way, g, d):
        values = [chunk(h, (1 - 2 * way) * d, o) for o in groups[g]]
        if d < hops_of(n, way, g):
            arrived(len(values), h, 2, plan[h, way, d + 1, g][0])
            values = add(values, h, way, d + 1, g)
        _, first, start = plan[h, way, d, g]
        for i, value in enumerate(values):
            q, scale = quantize(value)
            sn[start + i * high[h]:start + (i + 1) * high[h], :] = q
            cn[first + i:first + i + 1, :] = scale
        for copy in message(h, way, d, g):
            copy.start()

    def way_of(h, o):
        return 0 if o < n - o or (o == n - o and h == 0) else 1

    def target(h, o):
        hop = JUMPS[min(o, n - o)]
        return ((o - hop) % n, hop) if way_of(h, o) == 0 else ((o + hop) % n, -hop)

    def second(h, o):
        goals = sorted({target(h, b)[0] for b in range(1, n)})
        goal = m2_r.at[h, goals.index(target(h, o)[0])]
        to = along(1 - h, target(h, o)[1])
        row, rows = pl.ds(h * n + o, 1), pl.ds(begins[h] * span, high[h])
        return (remote(c2.at[row], rc2.at[row], 5, goal, to),
                remote(s2.at[o, rows], r2.at[o, rows], 3, goal, to))

    def own_step(h, g):
        values = [chunk(h, 0, o) for o in groups[g]]
        ways = [way for way in (0, 1) if hops_of(n, way, g) > 0]
        if ways:
            arrived(len(ways) * len(values), h, 2, last_r.at[h, g])
        for way in ways:
            values = add(values, h, way, 1, g)
        goals = sorted({target(h, b)[0] for b in range(1, n)})
        for value, o in zip(values, groups[g]):
            sources = [b for b in range(1, n) if target(h, b)[0] == o]
            if sources:
                arrived(len(sources), h, 3, m2_r.at[h, goals.index(o)])
            for b in sources:
                rows = slice(begins[h] * span, begins[h] * span + high[h])
                value = value + widen(r2[b, rows, :], rc2[h * n + b:h * n + b + 1, :])
            if o == 0:
                out[begins[h]:begins[h] + halves[h]] = (value * factor).reshape(halves[h], span, BLOCK)
            else:
                q, scale = quantize(value)
                s2[o, begins[h] * span:begins[h] * span + high[h], :] = q
                c2[h * n + o:h * n + o + 1, :] = scale
                for copy in second(h, o):
                    copy.start()

    run = {"near": near, "unit": products, "sum": step, "own": own_step}
    for op in order_of(n):
        run[op[0]](*op[1:])

    def sent(ref, i):
        remote(ref, ref, i, sib_r.at[0], {"dp": dp, "mp": sibling}).wait_send()

    for j in range(n):
        if nx > 1:
            sent(feats[j].at[pl.ds(0, 3 * nb)], 0)
        sent(feats[j].at[pl.ds(0, nb * nx)], 1)
    if n > 1:
        sent(sn, 2)
        sent(cn, 4)
        sent(s2.at[pl.ds(1, n - 1)], 3)
        sent(rc2.at[pl.ds(0, 2 * (n - 1))], 5)


def shards(n, nx, activations, out_grad, row_blocks, doc_lengths):
    slots = activations.shape[0]
    nb = activations.shape[1] // BLOCK
    columns, knz = row_blocks.shape
    first = FIRST if columns == 14 else columns // 2 - 1
    halves = (first, columns - first)
    factor = 1.0 / math.sqrt(slots * n * n)
    span = BLOCK // n
    sizes = [(len(group), hops_of(n, way, g)) for g, group in enumerate(groups_of(n)) for way in (0, 1) for h in (0, 1)]
    messages = max(1, sum(max(0, hops - 1) for _, hops in sizes))
    count = max(1, sum(hops * size for size, hops in sizes))
    depth = max(16, columns * span * sum(hops * size for size, hops in sizes) // 2)
    dma = pltpu.SemaphoreType.DMA
    operands = (activations, out_grad, row_blocks.T, doc_lengths)
    return pl.pallas_call(
        functools.partial(kernel, (n, nx, nb, knz, halves, factor)),
        out_shape=jax.ShapeDtypeStruct((columns, span * knz // n, BLOCK), jnp.float32),
        in_specs=[pl.BlockSpec(memory_space=pl.ANY)] * 4,
        out_specs=pl.BlockSpec(memory_space=pltpu.VMEM),
        scratch_shapes=[
            pltpu.VMEM(activations.shape, jnp.bfloat16),
            pltpu.VMEM(out_grad.shape, jnp.bfloat16),
            pltpu.SMEM(row_blocks.shape[::-1], jnp.int32),
            pltpu.SMEM(doc_lengths.shape, jnp.int32),
            pltpu.SMEM(row_blocks.shape[::-1], jnp.int32),
            pltpu.VMEM((nb, BLOCK, slots), jnp.bfloat16),
            pltpu.VMEM((columns, slots, BLOCK), jnp.bfloat16),
            pltpu.VMEM((n, knz, columns, span, BLOCK), jnp.float32),
            pltpu.VMEM((4, max(halves) * span // 2 + 1, BLOCK), jnp.float32),
            pltpu.VMEM((depth, BLOCK), jnp.int16),
            pltpu.VMEM((depth, BLOCK), jnp.int16),
            pltpu.VMEM((count, BLOCK), jnp.float32),
            pltpu.VMEM((count, BLOCK), jnp.float32),
            pltpu.VMEM((n, columns * span, BLOCK), jnp.int16),
            pltpu.VMEM((n, columns * span, BLOCK), jnp.int16),
            pltpu.VMEM((2 * n, BLOCK), jnp.float32),
            pltpu.VMEM((2 * n, BLOCK), jnp.float32),
            dma((4,)),
            dma((n,)),
            dma((n,)),
            dma((messages,)),
            dma((2, len(groups_of(n)))),
            dma((2, min(4, n))),
            dma((6,)),
        ] + [pltpu.VMEM((nb * nx * CORES, span, slots), jnp.bfloat16)] * n,
        compiler_params=pltpu.CompilerParams(
            collective_id=0, has_side_effects=True, vmem_limit_bytes=40 * 2**20),
    )(*(pltpu.with_memory_space_constraint(a, pltpu.HBM) for a in operands))


def solution(mesh):
    n = math.isqrt(mesh.shape["dp"])
    body = functools.partial(shards, n, mesh.shape["mp"] // CORES)
    in_specs = (P("dp", "mp"), P("dp", "mp"), P("mp", None), P("dp", None))
    return jax.shard_map(body, mesh=mesh, in_specs=in_specs, out_specs=P("mp", "dp", None), check_vma=False)
```
